128 devices in a mesh: gx: 4 (over x_lo, core), gy: 4 (over y), gz: 8 (over x_hi, z).
Axes of the slice: x: 4 (x_hi: 2, x_lo: 2; x = x_hi * 2 + x_lo), y: 4, z: 4, core: 2. Of those that a mesh axis runs over, the one named last changes fastest.
Arguments:
- positions: float32 [3, 2048, 128], P(None, ('gx', 'gy', 'gz')), may hold values from -6 to 6
- velocities: float32 [3, 2048, 128], P(None, ('gx', 'gy', 'gz')), may hold values from -6 to 6
- weights: float32 [2048, 128], P(('gx', 'gy', 'gz')), may hold values from 0.5 to 2
- counts: int32 [2048], P(('gx', 'gy', 'gz')), may hold values from 32 to 128
- link_offset: int32 [2048, 3], P(('gx', 'gy', 'gz')), may hold values from -16 to 16
- link_mask: int32 [2048, 3], P(('gx', 'gy', 'gz')), may hold values 0 or 1
- bin_box: int32 [2048, 1], P(('gx', 'gy', 'gz')), may hold values from 0 to 15; in each aligned block of 16 rows (0 to 15, 16 to 31, ...) at most 2 rows name the same one
- bin_cell: int32 [2048], P(('gx', 'gy', 'gz')), may hold values from 0 to 4095
- fluid: float32 [3, 16, 32, 1024], P(None, 'gx', 'gy', 'gz'), may hold values from -6 to 6
Outputs:
- positions_out: float32 [3, 2048, 128], P(None, ('gx', 'gy', 'gz'))
- velocities_out: float32 [3, 2048, 128], P(None, ('gx', 'gy', 'gz'))
- fluid_out: float32 [3, 16, 32, 1024], P(None, 'gx', 'gy', 'gz')
The draws below stay inside these ranges and needn't reach their ends.
Inputs may be any that keep to these rules, and one draw needn't show every extreme that they name: `bin_box`: the bins of one device name one value at most 2 times; the cell lies in the box at the bin owner's index of gz. `bin_cell`: index of the cell inside its box, first dimension slowest. Slots 0 to counts - 1 of a bin are occupied.
All inputs are finite; a program needn't handle non-finite values. No bound on the sum of `link_mask` on one device may be relied on, other than what follows from the above.
Results may differ from the reference program's by a relative error of at most 0.0001.
Values sent between devices are 32-bit elements; how exact they have to be, the bound alone decides.
A program may use at most 128 MiB of HBM per device.

```python
import math
import jax
import jax.numpy as jnp
import numpy as np
from jax import lax

S = 128
K_LINKS = 3
SUBSTEPS = 2
BIN_DEV = 16
CX = 4
CY = 8
CZ = 128
NB = 2048
BOX_SLOTS = 2
NX = 16
NY = 32
NZ = 1024
N_GX = 4
N_GY = 4
N_GZ = 8


def with_ends(drawn, key, low, high):
    extent = drawn.shape
    index_at = [jax.random.randint(jax.random.fold_in(key, axis), (), 0, extent[axis]) for axis in range(len(extent))]
    drawn = drawn.at[tuple(index_at)].set(low)
    longest = extent.index(max(extent))
    index_at[longest] = (index_at[longest] + 1) % extent[longest]
    return drawn.at[tuple(index_at)].set(high)


def block_levels(stream_key, dims, pieces, smallest, high):
    factor_of, own = 1.0, jax.random.fold_in(stream_key, 6)
    for axis_at, parts in pieces:
        heights = jnp.exp(jax.random.uniform(jax.random.fold_in(own, axis_at), (parts,), jnp.float32, smallest / len(pieces), high / len(pieces)))
        factor_of = factor_of * jnp.repeat(heights, dims[axis_at] // parts).reshape([-1 if axis == axis_at else 1 for axis in range(len(dims))])
    return factor_of


def deal_out(stream_key, own, number, rows, amount, top, most, slope):
    order = jax.random.permutation(stream_key, amount)
    heavy_load, ordinary = load_shares(amount, rows * top, most, slope, True), load_shares(amount, rows * top, most, slope, False)
    places = jnp.arange(amount)

    def named(sizes, rotation):
        used = int((sizes > 0).sum())
        fixed = max(1, used // 4)
        shifted = fixed + (places - fixed + rotation * (used - fixed)) % max(1, amount - fixed)
        return jnp.zeros((amount,), jnp.int32).at[order[jnp.where(places < fixed, places, shifted)]].set(jnp.asarray(sizes, jnp.int32))

    sizes = jnp.where(number % 4 == 0, named(heavy_load, number // 4), named(ordinary, number - number // 4 - 1))
    mixed = jax.random.permutation(jax.random.fold_in(own, 3), amount)
    giver, receiver = mixed[0:amount // 2 * 2:2], mixed[1:amount // 2 * 2:2]
    room = jnp.minimum(sizes[giver] - 1, most - sizes[receiver]) // 2
    room = jnp.where((giver == order[0]) | (receiver == order[0]) | (sizes[receiver] == 0), 0, jnp.maximum(room, 0))
    shifted = jax.random.randint(jax.random.fold_in(own, 4), (amount // 2,), 0, 1 << 20) % (room + 1)
    sizes = sizes.at[giver].add(-shifted).at[receiver].add(shifted)
    members = jnp.searchsorted(jnp.cumsum(sizes), jnp.arange(rows * top), side="right").astype(jnp.int32)
    listing = members.reshape(top, rows).T
    listing = listing[jax.random.permutation(jax.random.fold_in(own, 1), rows)]
    rotation = jax.random.randint(jax.random.fold_in(own, 2), (rows, 1), 0, top)
    return jnp.take_along_axis(listing, (jnp.arange(top)[None, :] + rotation) % top, axis=1)


def load_shares(count, total, bound, slope, full):
    loads = [(1 << 20) // math.isqrt(standing ** slope) + 1 for standing in range(1, count + 1)]
    largest = bound if full else min(bound, max(-(-total // count), total * loads[0] // sum(loads)))
    least = 1 if total - largest >= count - 1 else 0
    holding, spare = [largest] + [least] * (count - 1), total - largest - least * (count - 1)
    while spare > 0:
        movable = [i for i in range(1, count) if holding[i] < largest] or [i for i in range(1, count) if holding[i] < bound]
        whole, budget = sum([loads[i] for i in movable]), spare
        for i in movable:
            addition = min(bound - holding[i], max(1, budget * loads[i] // whole), spare)
            holding[i] = holding[i] + addition
            spare = spare - addition
    return np.array(holding)


def bell_draw(stream_key, extent, width, limit, pieces=(), kind=jnp.bfloat16):
    array = width * jax.random.normal(stream_key, extent, jnp.float32)
    if pieces:
        array = array * block_levels(stream_key, extent, pieces, -0.22, 0.18)
    return jnp.clip(array, -limit, limit).astype(kind)


def setup_inputs(seed: int = 0) -> dict:
    seeds = jax.random.split(jax.random.key(seed), 10)
    positions = bell_draw(seeds[0], (3, NB, S), 1.0, 6.0, ((1, 128),), jnp.float32)
    velocities = bell_draw(seeds[1], (3, NB, S), 1.0, 6.0, ((1, 128),), jnp.float32)
    weights = jnp.clip(jnp.exp(math.log(2.0) - 1.3862944 * jax.random.uniform(seeds[2], (NB, S), jnp.float32) ** block_levels(seeds[2], (NB, S), ((0, 128),), -0.2, 0.2)), 0.5, 2.0)
    counts = with_ends(jax.random.randint(seeds[3], (NB,), S // 4, S + 1), jax.random.fold_in(seeds[3], 1), S // 4, S).astype(jnp.int32)
    link_offset = with_ends(jax.random.randint(seeds[4], (NB, K_LINKS), 0 - BIN_DEV, BIN_DEV + 1), jax.random.fold_in(seeds[4], 1), 0 - BIN_DEV, BIN_DEV).astype(jnp.int32)
    link_mask = with_ends((jax.random.randint(seeds[5], (NB, K_LINKS), 0, 4) < 3).astype(jnp.int32), jax.random.fold_in(seeds[5], 1), 0, 1)
    bin_box_keys = jax.random.split(jax.random.fold_in(seeds[6], 1), NB // BIN_DEV)
    bin_box_turns = jax.random.permutation(jax.random.fold_in(seeds[6], 3), NB // BIN_DEV)
    bin_box = jax.vmap(lambda own, number: deal_out(jax.random.fold_in(seeds[6], 2), own, number, BIN_DEV, N_GX * N_GY, 1, BOX_SLOTS, 1))(bin_box_keys, bin_box_turns).reshape((NB, 1))
    bin_cell = with_ends(jax.random.randint(seeds[7], (NB,), 0, CX * CY * CZ), jax.random.fold_in(seeds[7], 1), 0, (CX * CY * CZ) - 1).astype(jnp.int32)
    fluid = bell_draw(seeds[8], (3, NX, NY, NZ), 1.0, 6.0, ((1, 4), (2, 4), (3, 8)), jnp.float32)
    return {"positions": positions, "velocities": velocities, "weights": weights, "counts": counts, "link_offset": link_offset, "link_mask": link_mask, "bin_box": bin_box, "bin_cell": bin_cell, "fluid": fluid}


step_sub = 0.1
stiffness = 0.05
damping = 0.05
drag_rate = 1.0
coupling = 0.004
viscosity = 0.12
highest = lax.Precision.HIGHEST


def contact(own_pos, own_vel, near_pos, near_vel, near_weight):
    distance = jnp.zeros(near_weight.shape[:2] + (own_pos.shape[2], near_weight.shape[2]), jnp.float32)
    for component in range(3):
        offset = own_pos[component][:, None, :, None] - near_pos[component][:, :, None, :]
        distance = distance + offset * offset
    kernel = near_weight[:, :, None, :] * jnp.exp(-0.5 * distance)
    weight_sum = jnp.sum(kernel, axis=(1, 3))
    pull_pos = jnp.einsum("bqij,cbqj->cbi", kernel, near_pos, precision=highest)
    pull_vel = jnp.einsum("bqij,cbqj->cbi", kernel, near_vel, precision=highest)
    return stiffness * (own_pos * weight_sum[None] - pull_pos) - damping * (own_vel * weight_sum[None] - pull_vel)


def advance(widened, state_pos, state_vel, carried, occupied, fluid_seen, neighbour, link_weight, block_bins):
    bin_count = state_pos.shape[1]

    def one_block(block_id, running):
        new_pos, new_vel, pulled = running
        first_bin = (block_id * block_bins).astype(jnp.int32)
        own_pos = lax.dynamic_slice_in_dim(state_pos, first_bin, block_bins, 1)
        own_vel = lax.dynamic_slice_in_dim(state_vel, first_bin, block_bins, 1)
        own_weight = lax.dynamic_slice_in_dim(carried, first_bin, block_bins, 0)
        own_occupied = lax.dynamic_slice_in_dim(occupied, first_bin, block_bins, 0)
        own_fluid = lax.dynamic_slice_in_dim(fluid_seen, first_bin, block_bins, 1)
        link_rows = lax.dynamic_slice_in_dim(neighbour, first_bin, block_bins, 0)
        link_block = lax.dynamic_slice_in_dim(link_weight, first_bin, block_bins, 0)
        nearby = widened[:, link_rows]
        near_pos = jnp.concatenate([own_pos[:, :, None], nearby[0:3]], 2)
        near_vel = jnp.concatenate([own_vel[:, :, None], nearby[3:6]], 2)
        near_weight = jnp.concatenate([own_weight[:, None], nearby[6] * link_block[:, :, None]], 1)
        contact_force = contact(own_pos, own_vel, near_pos, near_vel, near_weight)
        drag_force = drag_rate * (own_fluid[:, :, None] - own_vel)
        moved_vel = own_vel + step_sub * own_occupied[None] * (contact_force + drag_force)
        moved_pos = own_pos + step_sub * own_occupied[None] * moved_vel
        pulled_block = jnp.sum(own_weight[None] * drag_force, axis=2)
        new_pos = lax.dynamic_update_slice_in_dim(new_pos, moved_pos, first_bin, 1)
        new_vel = lax.dynamic_update_slice_in_dim(new_vel, moved_vel, first_bin, 1)
        pulled = lax.dynamic_update_slice_in_dim(pulled, pulled_block, first_bin, 1)
        return new_pos, new_vel, pulled

    start_state = (jnp.zeros_like(state_pos), jnp.zeros_like(state_vel), jnp.zeros((3, bin_count), jnp.float32))
    return lax.fori_loop(0, bin_count // block_bins, one_block, start_state)


def cell_coords(bin_box, bin_cell, bin_count):
    owner_dev = jnp.arange(bin_count, dtype=jnp.int32) // BIN_DEV
    height = owner_dev % N_GZ
    target = bin_box[:, 0]
    row_index = (target // N_GY) * CX + bin_cell // (CY * CZ)
    column_index = (target % N_GY) * CY + (bin_cell // CZ) % CY
    depth_index = height * CZ + bin_cell % CZ
    return row_index, column_index, depth_index


def laplace(velocity_field):
    padded = jnp.pad(velocity_field, ((0, 0), (1, 1), (1, 1), (1, 1)))
    centre = padded[:, 1:-1, 1:-1, 1:-1]
    beside_all = padded[:, 2:, 1:-1, 1:-1] + padded[:, :-2, 1:-1, 1:-1]
    beside_all = beside_all + padded[:, 1:-1, 2:, 1:-1] + padded[:, 1:-1, :-2, 1:-1]
    beside_all = beside_all + padded[:, 1:-1, 1:-1, 2:] + padded[:, 1:-1, 1:-1, :-2]
    return beside_all - 6.0 * centre


def reference(positions, velocities, weights, counts, link_offset, link_mask, bin_box, bin_cell, fluid):
    bin_count = positions.shape[1]
    slot_count = positions.shape[2]
    occupied = (jnp.arange(slot_count, dtype=jnp.int32)[None, :] < counts[:, None]).astype(jnp.float32)
    carried = weights * occupied
    row_index, column_index, depth_index = cell_coords(bin_box, bin_cell, bin_count)
    fluid_seen = fluid[:, row_index, column_index, depth_index]
    neighbour = jnp.arange(bin_count, dtype=jnp.int32)[:, None] + link_offset + BIN_DEV
    link_weight = link_mask.astype(jnp.float32)
    block_bins = 64 if bin_count % 64 == 0 else bin_count
    state_pos = positions
    state_vel = velocities
    pulled_total = jnp.zeros((3, bin_count), jnp.float32)
    for substep in range(SUBSTEPS):
        packed = jnp.concatenate([state_pos, state_vel, carried[None]], 0)
        widened = jnp.pad(packed, ((0, 0), (BIN_DEV, BIN_DEV), (0, 0)))
        state_pos, state_vel, pulled = advance(widened, state_pos, state_vel, carried, occupied, fluid_seen, neighbour, link_weight, block_bins)
        pulled_total = pulled_total + pulled
    source = jnp.zeros(fluid.shape, jnp.float32).at[:, row_index, column_index, depth_index].add(-coupling * pulled_total)
    first_rate = viscosity * laplace(fluid) + source
    middle = fluid + first_rate
    second_rate = viscosity * laplace(middle) + source
    fluid_out = fluid + 0.5 * (first_rate + second_rate)
    return state_pos, state_vel, fluid_out
```

```python
import functools

import jax
import jax.numpy as jnp
from jax import lax
from jax.experimental import pallas as pl
from jax.experimental.pallas import tpu as pltpu
from jax.sharding import PartitionSpec as P

f32, bf16, i32 = jnp.float32, jnp.bfloat16, jnp.int32
MESH = pl.DeviceIdType.MESH
BINS = 16
STEP, STIFF, DAMP, COUPLING, VISC = 0.1, 0.05, 0.05, 0.004, 0.12
ROOT_LOG2E = 1.4426950408889634**0.5


def iota(shape, dim):
    return lax.broadcasted_iota(i32, shape, dim)


def parts(x):
    high = x.astype(bf16).astype(f32)
    rest = x - high
    middle = rest.astype(bf16).astype(f32)
    return high, middle, rest - middle


def stacked(x):
    return jnp.concatenate([p.astype(bf16) for p in parts(x)], axis=0)


def kernel(
    sizes,
    pos,
    vel,
    wts,
    counts,
    loff,
    lmask,
    bbox,
    bcell,
    fluid,
    pos_out,
    vel_out,
    fluid_out,
    wide1,
    wide2,
    own_aug,
    aug,
    vals,
    sums,
    req,
    answer,
    ans,
    dep,
    lane_hot,
    row_hot,
    rate_buf,
    first_buf,
    hx,
    hy,
    hz,
    sy,
    sz,
    halo_send,
    halo_recv,
    group_send,
    group_recv,
    face_send,
    face_recv,
):
    ngx, ngy, ngz = sizes
    group, devices = ngx * ngy, ngx * ngy * ngz
    tiles = -(-group * BINS // 128)
    per_tile = 128 // BINS
    gx, gy, gz = (lax.axis_index(a) for a in ("gx", "gy", "gz"))
    me = gx * ngy + gy
    here = me * ngz + gz

    def in_group(g):
        return (lax.div(g, ngy), lax.rem(g, ngy), gz)

    def at(n):
        g = lax.div(n, ngz)
        return (lax.div(g, ngy), lax.rem(g, ngy), lax.rem(n, ngz))

    bin_right, bin_left = at(lax.rem(here + 1, devices)), at(lax.rem(here + devices - 1, devices))
    faces = (
        (lax.rem(gx + 1, ngx), gy, gz),
        (lax.rem(gx + ngx - 1, ngx), gy, gz),
        (gx, lax.rem(gy + 1, ngy), gz),
        (gx, lax.rem(gy + ngy - 1, ngy), gz),
        (gx, gy, lax.rem(gz + 1, ngz)),
        (gx, gy, lax.rem(gz + ngz - 1, ngz)),
    )

    barrier = pltpu.get_barrier_semaphore()

    @pl.loop(1, group)
    def _(k):
        pl.semaphore_signal(
            barrier, inc=1, device_id=in_group(lax.rem(me + k, group)), device_id_type=MESH
        )

    for other in (bin_right, bin_left, faces[4], faces[5]):
        pl.semaphore_signal(barrier, inc=1, device_id=other, device_id_type=MESH)

    row8, lane8 = iota((8, 128), 0), iota((8, 128), 1)
    row16, lane16 = iota((16, 128), 0), iota((16, 128), 1)

    for c in range(3):
        wide1[BINS : 2 * BINS, c, :] = pos[c]
        wide1[BINS : 2 * BINS, 3 + c, :] = vel[c]
    count_rows = jnp.zeros((16, 128), i32)
    asked = jnp.zeros((8, 128), i32)
    first_lane = lax.rem(me, per_tile) * BINS
    for b in range(BINS):
        count_rows = jnp.where(row16 == b, counts[b], count_rows)
        asked = jnp.where(
            lane8 == first_lane + b,
            jnp.where(row8 == 0, bbox[b, 0], jnp.where(row8 == 1, bcell[b], 0)),
            asked,
        )
    occupied = jnp.where(lane16 < count_rows, 1.0, 0.0).astype(f32)
    wide1[BINS : 2 * BINS, 6, :] = wts[...] * occupied
    wide1[BINS : 2 * BINS, 7, :] = occupied
    req[me] = asked

    def face_sources(turn, field):
        for side, (edge_row, edge_lane) in enumerate(((7, 127), (0, 0))):
            rows, lanes = jnp.zeros((16, 128), f32), jnp.zeros((8, 128), f32)
            for c in range(3):
                for x in range(4):
                    k = c * 4 + x
                    tile = field[c, x]
                    rows = jnp.where(row16 == k, tile[edge_row : edge_row + 1, :], rows)
                    lanes = jnp.where(lane8 == k, tile[:, edge_lane : edge_lane + 1], lanes)
            sy[turn, side] = rows
            sz[turn, side] = lanes

    def face_copies(turn, field):
        pairs = (
            (field.at[:, 3], hx.at[turn, 0]),
            (field.at[:, 0], hx.at[turn, 1]),
            (sy.at[turn, 0], hy.at[turn, 0]),
            (sy.at[turn, 1], hy.at[turn, 1]),
            (sz.at[turn, 0], hz.at[turn, 0]),
            (sz.at[turn, 1], hz.at[turn, 1]),
        )
        return [
            pltpu.make_async_remote_copy(
                src_ref=src,
                dst_ref=dst,
                send_sem=face_send.at[turn, n],
                recv_sem=face_recv.at[turn, n],
                device_id=faces[n],
                device_id_type=MESH,
            )
            for n, (src, dst) in enumerate(pairs)
        ]

    def halo_copies(turn, wide):
        own = wide.at[pl.ds(BINS, BINS)]
        return [
            pltpu.make_async_remote_copy(
                src_ref=own,
                dst_ref=wide.at[pl.ds(start, BINS)],
                send_sem=halo_send.at[turn, n],
                recv_sem=halo_recv.at[turn, n],
                device_id=other,
                device_id_type=MESH,
            )
            for n, (start, other) in enumerate(((0, bin_right), (2 * BINS, bin_left)))
        ]

    def group_copy(turn, src, dst, other):
        return pltpu.make_async_remote_copy(
            src_ref=src,
            dst_ref=dst,
            send_sem=group_send.at[turn],
            recv_sem=group_recv.at[turn],
            device_id=other,
            device_id_type=MESH,
        )

    def group_start(turn, buffer, source):
        @pl.loop(1, group)
        def _(k):
            other = lax.rem(me + k, group)
            group_copy(turn, source(other), buffer.at[me], in_group(other)).start()

    def group_all(turn, buffer):
        most = buffer.at[pl.ds(0, group - 1)]
        return group_copy(turn, most, most, in_group(lax.rem(me + 1, group)))

    def gathered(buffer):
        out = []
        for t in range(tiles):
            total = buffer[t * per_tile]
            for s in range(t * per_tile + 1, min(group, (t + 1) * per_tile)):
                total = total + buffer[s]
            out.append(total)
        return jnp.concatenate(out, axis=1) if tiles > 1 else out[0]

    face_sources(0, fluid)
    pl.semaphore_wait(barrier, group - 1 + 4)

    group_start(0, req, lambda other: req.at[me])
    halo1 = halo_copies(0, wide1)
    for copy in halo1:
        copy.start()
    faces0 = face_copies(0, fluid)
    for copy in faces0:
        copy.start()

    def prepare(wide, slot, scale, own):
        tile = wide[slot]
        carried = tile[6:7, :] * scale
        v = jnp.where(row8 < 6, tile, jnp.where(row8 == 6, 1.0, 0.0)) * carried
        vh, vm, vl = parts(v)
        vals[slot] = jnp.concatenate([vh, vm, vl, jnp.zeros_like(vh)], axis=0).astype(bf16)
        y = jnp.where(row8 < 3, tile * ROOT_LOG2E, 0.0)
        norm = -0.5 * jnp.sum(y * y, axis=0, keepdims=True)
        h, m, l = parts(jnp.where(row8 == 3, norm, y))
        ones = jnp.where((row8 >= 4) & (row8 < 7), 1.0, h)
        aug[slot] = jnp.concatenate([ones, m, l, h, m, h], axis=0).astype(bf16)
        if own:
            high = jnp.where(row8 < 3, h, jnp.where(row8 == 3, 1.0, 0.0))
            low = jnp.where(row8 < 3, m, 0.0)
            lowest = jnp.where(row8 < 3, l, 0.0)
            norms = jnp.where(
                row8 == 4,
                h[3:4, :],
                jnp.where(row8 == 5, m[3:4, :], jnp.where(row8 == 6, l[3:4, :], high)),
            )
            own_aug[slot - BINS] = jnp.concatenate(
                [norms, high, high, low, low, lowest], axis=0
            ).astype(bf16)

    def prepare_own(wide):
        @pl.loop(BINS, 2 * BINS)
        def _(slot):
            prepare(wide, slot, 1.0, True)

    has_left = jnp.where(here > 0, 1.0, 0.0).astype(f32)
    has_right = jnp.where(here < devices - 1, 1.0, 0.0).astype(f32)

    def prepare_halo(wide):
        @pl.loop(0, BINS)
        def _(slot):
            prepare(wide, slot, has_left, False)
            prepare(wide, slot + 2 * BINS, has_right, False)

    def contact(b):
        slots = [b + BINS]
        for q in range(3):
            slots.append(jnp.where(lmask[b, q] != 0, b + BINS + loff[b, q], 3 * BINS))
        near = jnp.concatenate([aug[s] for s in slots], axis=1)
        value = jnp.concatenate([vals[s] for s in slots], axis=1)
        exponent = lax.dot_general(
            own_aug[b], near, (((0,), (0,)), ((), ())), preferred_element_type=f32
        )
        pair = jnp.exp2(exponent)
        high = pair.astype(bf16)
        low = (pair - high.astype(f32)).astype(bf16)
        by_pair = (((1,), (1,)), ((), ()))
        total = lax.dot_general(value, high, by_pair, preferred_element_type=f32)
        total = total + lax.dot_general(value, low, by_pair, preferred_element_type=f32)
        return total[0:8] + total[8:16] + total[16:24]

    def advanced(tile, total, seen):
        net = tile * total[6:7, :] - total
        force = STIFF * pltpu.roll(net, 3, 0) - DAMP * net
        held = STEP * tile[7:8, :]
        new_v = tile + held * (force + (seen - tile))
        new_x = tile + held * pltpu.roll(new_v, 5, 0)
        return jnp.where(row8 < 3, new_x, jnp.where(row8 < 6, new_v, tile))

    aug[3 * BINS] = jnp.zeros((48, 128), bf16)
    vals[3 * BINS] = jnp.zeros((32, 128), bf16)
    prepare_own(wide1)

    group_all(0, req).wait_recv()
    asked_all = gathered(req)
    wide_lanes = 128 * tiles
    cell = asked_all[1:2, :]
    lane_hot[...] = jnp.where(
        iota((128, wide_lanes), 0) == (cell & 127), 1.0, 0.0
    ).astype(bf16)
    row_hot[...] = jnp.where(
        (iota((32, wide_lanes), 0) == (cell >> 7)) & (asked_all[0:1, :] == me), 1.0, 0.0
    ).astype(f32)
    at_lane = jnp.dot(
        stacked(fluid[...].reshape(96, 128)), lane_hot[...], preferred_element_type=f32
    )
    at_lane = at_lane[0:96] + at_lane[96:192] + at_lane[192:288]
    reply = jnp.zeros((8, wide_lanes), f32)
    wide_row = iota((8, wide_lanes), 0)
    for c in range(3):
        picked = jnp.sum(at_lane[32 * c : 32 * c + 32] * row_hot[...], axis=0, keepdims=True)
        reply = jnp.where(wide_row == 3 + c, picked, reply)
    for t in range(tiles):
        answer[t] = reply[:, 128 * t : 128 * t + 128]
    ans[me] = answer[lax.div(me, per_tile)]
    group_start(1, ans, lambda other: answer.at[lax.div(other, per_tile)])

    in_x = [jnp.where(g, 1.0, 0.0).astype(f32) for g in (gx > 0, gx < ngx - 1)]
    in_y = [jnp.where(g, 1.0, 0.0).astype(f32) for g in (gy > 0, gy < ngy - 1)]
    in_z = [jnp.where(g, 1.0, 0.0).astype(f32) for g in (gz > 0, gz < ngz - 1)]

    def laplace(turn, field, c, x):
        k = c * 4 + x
        tile = field[c, x]
        below = field[c, x - 1] if x > 0 else hx[turn, 0, c] * in_x[0]
        above = field[c, x + 1] if x < 3 else hx[turn, 1, c] * in_x[1]
        total = below + above - 6.0 * tile
        total = total + jnp.where(
            row8 == 0, hy[turn, 0, k : k + 1, :] * in_y[0], pltpu.roll(tile, 1, 0)
        )
        total = total + jnp.where(
            row8 == 7, hy[turn, 1, k : k + 1, :] * in_y[1], pltpu.roll(tile, 7, 0)
        )
        zl, zr = hz[turn, 0] * in_z[0], hz[turn, 1] * in_z[1]
        total = total + jnp.where(lane8 == 0, zl[:, k : k + 1], pltpu.roll(tile, 1, 1))
        return total + jnp.where(lane8 == 127, zr[:, k : k + 1], pltpu.roll(tile, 127, 1))

    for copy in faces0:
        copy.wait_recv()
    for c in range(3):
        for x in range(4):
            rate_buf[c, x] = VISC * laplace(0, fluid, c, x)

    for copy in halo1:
        copy.wait_recv()
    prepare_halo(wide1)

    @pl.loop(0, BINS, unroll=4)
    def _(b):
        sums[b] = contact(b)

    group_all(1, ans).wait_recv()
    seen = ans[0]
    for s in range(1, group):
        seen = seen + ans[s]
    seen = pltpu.roll(seen, lax.rem(128 - first_lane, 128), 1)
    drawn = jnp.zeros((8, 128), f32)
    for b in range(BINS):
        seen_b = jnp.broadcast_to(seen[:, b : b + 1], (8, 128))
        tile = wide1[BINS + b]
        new = advanced(tile, sums[b], seen_b)
        wide2[BINS + b] = new
        drag = (seen_b - tile) + (seen_b - new)
        pulled = jnp.sum(tile[6:7, :] * drag, axis=1, keepdims=True)
        drawn = jnp.where(lane8 == b, pulled, drawn)
    dep[me] = pltpu.roll(drawn, first_lane, 1)
    halo2 = halo_copies(1, wide2)
    for copy in halo2:
        copy.start()
    group_start(2, dep, lambda other: dep.at[me])
    prepare_own(wide2)

    group_all(2, dep).wait_recv()
    pushed = -COUPLING * gathered(dep)
    spread = jnp.concatenate(
        [pushed[3 + c : 4 + c, :] * row_hot[...] for c in range(3)], axis=0
    )
    source = lax.dot_general(
        stacked(spread), lane_hot[...], (((1,), (1,)), ((), ())), preferred_element_type=f32
    )
    source = source[0:96] + source[96:192] + source[192:288]
    first_buf[...] = rate_buf[...] + source.reshape(3, 4, 8, 128)
    face_sources(1, first_buf)
    faces1 = face_copies(1, first_buf)
    for copy in faces1:
        copy.start()

    for copy in halo2:
        copy.wait_recv()
    prepare_halo(wide2)

    @pl.loop(0, BINS, unroll=4)
    def _(b):
        sums[b] = contact(b)

    for b in range(BINS):
        sums[b] = advanced(
            wide2[BINS + b], sums[b], jnp.broadcast_to(seen[:, b : b + 1], (8, 128))
        )
    for c in range(3):
        pos_out[c] = sums[:, c, :]
        vel_out[c] = sums[:, 3 + c, :]

    for copy in faces1:
        copy.wait_recv()
    for c in range(3):
        for x in range(4):
            fluid_out[c, x] = (
                fluid[c, x] + first_buf[c, x] + (0.5 * VISC) * laplace(1, first_buf, c, x)
            )

    for copy in (*halo1, *faces0, *halo2, *faces1):
        copy.wait_send()
    for turn, buffer in enumerate((req, ans, dep)):
        group_all(turn, buffer).wait_send()


def local(sizes, *args):
    group = sizes[0] * sizes[1]
    tiles = -(-group * BINS // 128)
    vmem, smem = pl.BlockSpec(memory_space=pltpu.VMEM), pl.BlockSpec(memory_space=pltpu.SMEM)
    dma = pltpu.SemaphoreType.DMA
    return tuple(
        pl.pallas_call(
            functools.partial(kernel, sizes),
            out_shape=(
                jax.ShapeDtypeStruct((3, BINS, 128), f32),
                jax.ShapeDtypeStruct((3, BINS, 128), f32),
                jax.ShapeDtypeStruct((3, 4, 8, 128), f32),
            ),
            in_specs=[vmem] * 3 + [smem] * 5 + [vmem],
            out_specs=(vmem,) * 3,
            scratch_shapes=[
                pltpu.VMEM((3 * BINS, 8, 128), f32),
                pltpu.VMEM((3 * BINS, 8, 128), f32),
                pltpu.VMEM((BINS, 48, 128), bf16),
                pltpu.VMEM((3 * BINS + 1, 48, 128), bf16),
                pltpu.VMEM((3 * BINS + 1, 32, 128), bf16),
                pltpu.VMEM((BINS, 8, 128), f32),
                pltpu.VMEM((group, 8, 128), i32),
                pltpu.VMEM((tiles, 8, 128), f32),
                pltpu.VMEM((group, 8, 128), f32),
                pltpu.VMEM((group, 8, 128), f32),
                pltpu.VMEM((128, 128 * tiles), bf16),
                pltpu.VMEM((32, 128 * tiles), f32),
                pltpu.VMEM((3, 4, 8, 128), f32),
                pltpu.VMEM((3, 4, 8, 128), f32),
                pltpu.VMEM((2, 2, 3, 8, 128), f32),
                pltpu.VMEM((2, 2, 16, 128), f32),
                pltpu.VMEM((2, 2, 8, 128), f32),
                pltpu.VMEM((2, 2, 16, 128), f32),
                pltpu.VMEM((2, 2, 8, 128), f32),
                dma((2, 2)),
                dma((2, 2)),
                dma((3,)),
                dma((3,)),
                dma((2, 6)),
                dma((2, 6)),
            ],
            compiler_params=pltpu.CompilerParams(
                collective_id=0, has_side_effects=True, vmem_limit_bytes=16 * 2**20
            ),
            name="bed_step",
        )(*args)
    )


def solution(mesh):
    sizes = tuple(mesh.shape[a] for a in ("gx", "gy", "gz"))
    bins = ("gx", "gy", "gz")
    in_specs = (
        P(None, bins, None),
        P(None, bins, None),
        P(bins, None),
        P(bins),
        P(bins, None),
        P(bins, None),
        P(bins, None),
        P(bins),
        P(None, "gx", "gy", "gz"),
    )
    out_specs = (P(None, bins, None), P(None, bins, None), P(None, "gx", "gy", "gz"))
    return jax.shard_map(
        functools.partial(local, sizes),
        mesh=mesh,
        in_specs=in_specs,
        out_specs=out_specs,
        check_vma=False,
    )
```

```python
import functools

import jax
import jax.numpy as jnp
from jax import lax
from jax.experimental import pallas as pl
from jax.experimental.pallas import tpu as pltpu
from jax.sharding import PartitionSpec as P

f32, bf16, i32 = jnp.float32, jnp.bfloat16, jnp.int32
MESH = pl.DeviceIdType.MESH
BINS = 16
STEP, STIFF, DAMP, COUPLING, VISC = 0.1, 0.05, 0.05, 0.004, 0.12
ROOT_LOG2E = 1.4426950408889634**0.5


def iota(shape, dim):
    return lax.broadcasted_iota(i32, shape, dim)


def parts(x):
    high = x.astype(bf16).astype(f32)
    rest = x - high
    middle = rest.astype(bf16).astype(f32)
    return high, middle, rest - middle


def stacked(x):
    return jnp.concatenate([p.astype(bf16) for p in parts(x)], axis=0)


def kernel(
    sizes,
    pos_in,
    vel_in,
    wts_in,
    counts_in,
    loff_in,
    lmask_in,
    bbox_in,
    bcell_in,
    fluid_in,
    pos_out,
    vel_out,
    fluid_out,
    pos,
    vel,
    wts,
    counts,
    loff,
    lmask,
    bbox,
    bcell,
    fluid,
    wide1,
    wide2,
    own_aug,
    aug,
    vals,
    sums,
    req,
    answer,
    ans,
    dep,
    lane_hot,
    row_hot,
    rate_buf,
    first_buf,
    hx,
    hy,
    hz,
    sy,
    sz,
    load_sem,
    halo_send,
    halo_recv,
    group_send,
    group_recv,
    face_send,
    face_recv,
):
    ngx, ngy, ngz = sizes
    group, devices = ngx * ngy, ngx * ngy * ngz
    tiles = -(-group * BINS // 128)
    per_tile = 128 // BINS
    gx, gy, gz = (lax.axis_index(a) for a in ("gx", "gy", "gz"))
    me = gx * ngy + gy
    here = me * ngz + gz

    def in_group(g):
        return (lax.div(g, ngy), lax.rem(g, ngy), gz)

    def at(n):
        g = lax.div(n, ngz)
        return (lax.div(g, ngy), lax.rem(g, ngy), lax.rem(n, ngz))

    bin_right, bin_left = at(lax.rem(here + 1, devices)), at(lax.rem(here + devices - 1, devices))
    faces = (
        (lax.rem(gx + 1, ngx), gy, gz),
        (lax.rem(gx + ngx - 1, ngx), gy, gz),
        (gx, lax.rem(gy + 1, ngy), gz),
        (gx, lax.rem(gy + ngy - 1, ngy), gz),
        (gx, gy, lax.rem(gz + 1, ngz)),
        (gx, gy, lax.rem(gz + ngz - 1, ngz)),
    )

    loads = [
        pltpu.make_async_copy(src, dst, load_sem.at[n])
        for n, (src, dst) in enumerate(
            (
                (bbox_in, bbox),
                (bcell_in, bcell),
                (fluid_in, fluid),
                (pos_in, pos),
                (vel_in, vel),
                (counts_in, counts),
                (wts_in, wts),
                (loff_in, loff),
                (lmask_in, lmask),
            )
        )
    ]
    for copy in loads:
        copy.start()

    barrier = pltpu.get_barrier_semaphore()

    @pl.loop(1, group)
    def _(k):
        pl.semaphore_signal(
            barrier, inc=1, device_id=in_group(lax.rem(me + k, group)), device_id_type=MESH
        )

    for other in (bin_right, bin_left, faces[4], faces[5]):
        pl.semaphore_signal(barrier, inc=1, device_id=other, device_id_type=MESH)

    row8, lane8 = iota((8, 128), 0), iota((8, 128), 1)
    row16, lane16 = iota((16, 128), 0), iota((16, 128), 1)

    loads[0].wait()
    loads[1].wait()
    asked = jnp.zeros((8, 128), i32)
    first_lane = lax.rem(me, per_tile) * BINS
    for b in range(BINS):
        asked = jnp.where(
            lane8 == first_lane + b,
            jnp.where(row8 == 0, bbox[0, b], jnp.where(row8 == 1, bcell[b], 0)),
            asked,
        )
    req[me] = asked

    def face_sources(turn, field):
        for side, (edge_row, edge_lane) in enumerate(((7, 127), (0, 0))):
            rows, lanes = jnp.zeros((16, 128), f32), jnp.zeros((8, 128), f32)
            for c in range(3):
                for x in range(4):
                    k = c * 4 + x
                    tile = field[c, x]
                    rows = jnp.where(row16 == k, tile[edge_row : edge_row + 1, :], rows)
                    lanes = jnp.where(lane8 == k, tile[:, edge_lane : edge_lane + 1], lanes)
            sy[turn, side] = rows
            sz[turn, side] = lanes

    def face_copies(turn, field):
        pairs = (
            (field.at[:, 3], hx.at[turn, 0]),
            (field.at[:, 0], hx.at[turn, 1]),
            (sy.at[turn, 0], hy.at[turn, 0]),
            (sy.at[turn, 1], hy.at[turn, 1]),
            (sz.at[turn, 0], hz.at[turn, 0]),
            (sz.at[turn, 1], hz.at[turn, 1]),
        )
        return [
            pltpu.make_async_remote_copy(
                src_ref=src,
                dst_ref=dst,
                send_sem=face_send.at[turn, n],
                recv_sem=face_recv.at[turn, n],
                device_id=faces[n],
                device_id_type=MESH,
            )
            for n, (src, dst) in enumerate(pairs)
        ]

    def halo_copies(turn, wide):
        own = wide.at[pl.ds(BINS, BINS)]
        return [
            pltpu.make_async_remote_copy(
                src_ref=own,
                dst_ref=wide.at[pl.ds(start, BINS)],
                send_sem=halo_send.at[turn, n],
                recv_sem=halo_recv.at[turn, n],
                device_id=other,
                device_id_type=MESH,
            )
            for n, (start, other) in enumerate(((0, bin_right), (2 * BINS, bin_left)))
        ]

    def group_copy(turn, src, dst, other):
        return pltpu.make_async_remote_copy(
            src_ref=src,
            dst_ref=dst,
            send_sem=group_send.at[turn],
            recv_sem=group_recv.at[turn],
            device_id=other,
            device_id_type=MESH,
        )

    def group_start(turn, buffer, source):
        @pl.loop(1, group)
        def _(k):
            other = lax.rem(me + k, group)
            group_copy(turn, source(other), buffer.at[me], in_group(other)).start()

    def group_all(turn, buffer):
        most = buffer.at[pl.ds(0, group - 1)]
        return group_copy(turn, most, most, in_group(lax.rem(me + 1, group)))

    def gathered(buffer):
        out = []
        for t in range(tiles):
            total = buffer[t * per_tile]
            for s in range(t * per_tile + 1, min(group, (t + 1) * per_tile)):
                total = total + buffer[s]
            out.append(total)
        return jnp.concatenate(out, axis=1) if tiles > 1 else out[0]

    loads[2].wait()
    face_sources(0, fluid)

    for copy in loads[3:]:
        copy.wait()
    for c in range(3):
        wide1[BINS : 2 * BINS, c, :] = pos[c]
        wide1[BINS : 2 * BINS, 3 + c, :] = vel[c]
    count_rows = jnp.zeros((16, 128), i32)
    for b in range(BINS):
        count_rows = jnp.where(row16 == b, counts[b], count_rows)
    occupied = jnp.where(lane16 < count_rows, 1.0, 0.0).astype(f32)
    wide1[BINS : 2 * BINS, 6, :] = wts[...] * occupied
    wide1[BINS : 2 * BINS, 7, :] = occupied

    pl.semaphore_wait(barrier, group - 1 + 4)

    group_start(0, req, lambda other: req.at[me])
    halo1 = halo_copies(0, wide1)
    for copy in halo1:
        copy.start()
    faces0 = face_copies(0, fluid)
    for copy in faces0:
        copy.start()

    def prepare(wide, slot, scale, own):
        tile = wide[slot]
        carried = tile[6:7, :] * scale
        v = jnp.where(row8 < 6, tile, jnp.where(row8 == 6, 1.0, 0.0)) * carried
        vh, vm, vl = parts(v)
        vals[slot] = jnp.concatenate([vh, vm, vl, jnp.zeros_like(vh)], axis=0).astype(bf16)
        y = jnp.where(row8 < 3, tile * ROOT_LOG2E, 0.0)
        norm = -0.5 * jnp.sum(y * y, axis=0, keepdims=True)
        h, m, l = parts(jnp.where(row8 == 3, norm, y))
        ones = jnp.where((row8 >= 4) & (row8 < 7), 1.0, h)
        aug[slot] = jnp.concatenate([ones, m, l, h, m, h], axis=0).astype(bf16)
        if own:
            high = jnp.where(row8 < 3, h, jnp.where(row8 == 3, 1.0, 0.0))
            low = jnp.where(row8 < 3, m, 0.0)
            lowest = jnp.where(row8 < 3, l, 0.0)
            norms = jnp.where(
                row8 == 4,
                h[3:4, :],
                jnp.where(row8 == 5, m[3:4, :], jnp.where(row8 == 6, l[3:4, :], high)),
            )
            own_aug[slot - BINS] = jnp.concatenate(
                [norms, high, high, low, low, lowest], axis=0
            ).astype(bf16)

    def prepare_own(wide):
        @pl.loop(BINS, 2 * BINS)
        def _(slot):
            prepare(wide, slot, 1.0, True)

    has_left = jnp.where(here > 0, 1.0, 0.0).astype(f32)
    has_right = jnp.where(here < devices - 1, 1.0, 0.0).astype(f32)

    def prepare_halo(wide):
        @pl.loop(0, BINS)
        def _(slot):
            prepare(wide, slot, has_left, False)
            prepare(wide, slot + 2 * BINS, has_right, False)

    def contact(b):
        slots = [b + BINS]
        for q in range(3):
            slots.append(jnp.where(lmask[q, b] != 0, b + BINS + loff[q, b], 3 * BINS))
        near = jnp.concatenate([aug[s] for s in slots], axis=1)
        value = jnp.concatenate([vals[s] for s in slots], axis=1)
        exponent = lax.dot_general(
            near, own_aug[b], (((0,), (0,)), ((), ())), preferred_element_type=f32
        )
        pair = jnp.exp2(exponent)
        high = pair.astype(bf16)
        low = (pair - high.astype(f32)).astype(bf16)
        total = jnp.dot(value, high, preferred_element_type=f32)
        total = total + jnp.dot(value, low, preferred_element_type=f32)
        return total[0:8] + total[8:16] + total[16:24]

    def advanced(tile, total, seen):
        net = tile * total[6:7, :] - total
        force = STIFF * pltpu.roll(net, 3, 0) - DAMP * net
        held = STEP * tile[7:8, :]
        new_v = tile + held * (force + (seen - tile))
        new_x = tile + held * pltpu.roll(new_v, 5, 0)
        return jnp.where(row8 < 3, new_x, jnp.where(row8 < 6, new_v, tile))

    aug[3 * BINS] = jnp.zeros((48, 128), bf16)
    vals[3 * BINS] = jnp.zeros((32, 128), bf16)
    prepare_own(wide1)

    group_all(0, req).wait_recv()
    asked_all = gathered(req)
    wide_lanes = 128 * tiles
    cell = asked_all[1:2, :]
    lane_hot[...] = jnp.where(
        iota((128, wide_lanes), 0) == (cell & 127), 1.0, 0.0
    ).astype(bf16)
    row_hot[...] = jnp.where(
        (iota((32, wide_lanes), 0) == (cell >> 7)) & (asked_all[0:1, :] == me), 1.0, 0.0
    ).astype(f32)
    at_lane = jnp.dot(
        stacked(fluid[...].reshape(96, 128)), lane_hot[...], preferred_element_type=f32
    )
    at_lane = at_lane[0:96] + at_lane[96:192] + at_lane[192:288]
    reply = jnp.zeros((8, wide_lanes), f32)
    wide_row = iota((8, wide_lanes), 0)
    for c in range(3):
        picked = jnp.sum(at_lane[32 * c : 32 * c + 32] * row_hot[...], axis=0, keepdims=True)
        reply = jnp.where(wide_row == 3 + c, picked, reply)
    for t in range(tiles):
        answer[t] = reply[:, 128 * t : 128 * t + 128]
    ans[me] = answer[lax.div(me, per_tile)]
    group_start(1, ans, lambda other: answer.at[lax.div(other, per_tile)])

    in_x = [jnp.where(g, 1.0, 0.0).astype(f32) for g in (gx > 0, gx < ngx - 1)]
    in_y = [jnp.where(g, 1.0, 0.0).astype(f32) for g in (gy > 0, gy < ngy - 1)]
    in_z = [jnp.where(g, 1.0, 0.0).astype(f32) for g in (gz > 0, gz < ngz - 1)]

    def laplace(turn, field, c, x):
        k = c * 4 + x
        tile = field[c, x]
        below = field[c, x - 1] if x > 0 else hx[turn, 0, c] * in_x[0]
        above = field[c, x + 1] if x < 3 else hx[turn, 1, c] * in_x[1]
        total = below + above - 6.0 * tile
        total = total + jnp.where(
            row8 == 0, hy[turn, 0, k : k + 1, :] * in_y[0], pltpu.roll(tile, 1, 0)
        )
        total = total + jnp.where(
            row8 == 7, hy[turn, 1, k : k + 1, :] * in_y[1], pltpu.roll(tile, 7, 0)
        )
        zl, zr = hz[turn, 0] * in_z[0], hz[turn, 1] * in_z[1]
        total = total + jnp.where(lane8 == 0, zl[:, k : k + 1], pltpu.roll(tile, 1, 1))
        return total + jnp.where(lane8 == 127, zr[:, k : k + 1], pltpu.roll(tile, 127, 1))

    for copy in faces0:
        copy.wait_recv()
    for c in range(3):
        for x in range(4):
            rate_buf[c, x] = VISC * laplace(0, fluid, c, x)

    for copy in halo1:
        copy.wait_recv()
    prepare_halo(wide1)

    @pl.loop(0, BINS, unroll=8)
    def _(b):
        sums[b] = contact(b)

    group_all(1, ans).wait_recv()
    seen = ans[0]
    for s in range(1, group):
        seen = seen + ans[s]
    seen = pltpu.roll(seen, lax.rem(128 - first_lane, 128), 1)
    drawn = jnp.zeros((8, 128), f32)
    for b in range(BINS):
        seen_b = jnp.broadcast_to(seen[:, b : b + 1], (8, 128))
        tile = wide1[BINS + b]
        new = advanced(tile, sums[b], seen_b)
        wide2[BINS + b] = new
        drag = (seen_b - tile) + (seen_b - new)
        pulled = jnp.sum(tile[6:7, :] * drag, axis=1, keepdims=True)
        drawn = jnp.where(lane8 == b, pulled, drawn)
    dep[me] = pltpu.roll(drawn, first_lane, 1)
    halo2 = halo_copies(1, wide2)
    for copy in halo2:
        copy.start()
    group_start(2, dep, lambda other: dep.at[me])
    prepare_own(wide2)

    group_all(2, dep).wait_recv()
    pushed = -COUPLING * gathered(dep)
    spread = jnp.concatenate(
        [pushed[3 + c : 4 + c, :] * row_hot[...] for c in range(3)], axis=0
    )
    source = lax.dot_general(
        stacked(spread), lane_hot[...], (((1,), (1,)), ((), ())), preferred_element_type=f32
    )
    source = source[0:96] + source[96:192] + source[192:288]
    first_buf[...] = rate_buf[...] + source.reshape(3, 4, 8, 128)
    face_sources(1, first_buf)
    faces1 = face_copies(1, first_buf)
    for copy in faces1:
        copy.start()

    for copy in halo2:
        copy.wait_recv()
    prepare_halo(wide2)

    @pl.loop(0, BINS, unroll=8)
    def _(b):
        sums[b] = contact(b)

    for b in range(BINS):
        sums[b] = advanced(
            wide2[BINS + b], sums[b], jnp.broadcast_to(seen[:, b : b + 1], (8, 128))
        )
    for c in range(3):
        pos_out[c] = sums[:, c, :]
        vel_out[c] = sums[:, 3 + c, :]

    for copy in faces1:
        copy.wait_recv()
    for c in range(3):
        for x in range(4):
            fluid_out[c, x] = (
                fluid[c, x] + first_buf[c, x] + (0.5 * VISC) * laplace(1, first_buf, c, x)
            )

    for copy in (*halo1, *faces0, *halo2, *faces1):
        copy.wait_send()
    for turn, buffer in enumerate((req, ans, dep)):
        group_all(turn, buffer).wait_send()


def write_out(*refs):
    sems = refs[-1]
    copies = [pltpu.make_async_copy(refs[n], refs[3 + n], sems.at[n]) for n in range(3)]
    for copy in copies:
        copy.start()
    for copy in copies:
        copy.wait()


def local(sizes, pos, vel, wts, counts, loff, lmask, bbox, bcell, fluid):
    group = sizes[0] * sizes[1]
    tiles = -(-group * BINS // 128)
    vmem, anywhere = pl.BlockSpec(memory_space=pltpu.VMEM), pl.BlockSpec(memory_space=pltpu.HBM)
    dma = pltpu.SemaphoreType.DMA
    out_shape = (
        jax.ShapeDtypeStruct((3, BINS, 128), f32),
        jax.ShapeDtypeStruct((3, BINS, 128), f32),
        jax.ShapeDtypeStruct((3, 4, 8, 128), f32),
    )
    results = pl.pallas_call(
            functools.partial(kernel, sizes),
            out_shape=out_shape,
            in_specs=[anywhere] * 9,
            out_specs=(vmem,) * 3,
            scratch_shapes=[
                pltpu.VMEM((3, BINS, 128), f32),
                pltpu.VMEM((3, BINS, 128), f32),
                pltpu.VMEM((BINS, 128), f32),
                pltpu.SMEM((BINS,), i32),
                pltpu.SMEM((3, BINS), i32),
                pltpu.SMEM((3, BINS), i32),
                pltpu.SMEM((1, BINS), i32),
                pltpu.SMEM((BINS,), i32),
                pltpu.VMEM((3, 4, 8, 128), f32),
                pltpu.VMEM((3 * BINS, 8, 128), f32),
                pltpu.VMEM((3 * BINS, 8, 128), f32),
                pltpu.VMEM((BINS, 48, 128), bf16),
                pltpu.VMEM((3 * BINS + 1, 48, 128), bf16),
                pltpu.VMEM((3 * BINS + 1, 32, 128), bf16),
                pltpu.VMEM((BINS, 8, 128), f32),
                pltpu.VMEM((group, 8, 128), i32),
                pltpu.VMEM((tiles, 8, 128), f32),
                pltpu.VMEM((group, 8, 128), f32),
                pltpu.VMEM((group, 8, 128), f32),
                pltpu.VMEM((128, 128 * tiles), bf16),
                pltpu.VMEM((32, 128 * tiles), f32),
                pltpu.VMEM((3, 4, 8, 128), f32),
                pltpu.VMEM((3, 4, 8, 128), f32),
                pltpu.VMEM((2, 2, 3, 8, 128), f32),
                pltpu.VMEM((2, 2, 16, 128), f32),
                pltpu.VMEM((2, 2, 8, 128), f32),
                pltpu.VMEM((2, 2, 16, 128), f32),
                pltpu.VMEM((2, 2, 8, 128), f32),
                dma((9,)),
                dma((2, 2)),
                dma((2, 2)),
                dma((3,)),
                dma((3,)),
                dma((2, 6)),
                dma((2, 6)),
            ],
            compiler_params=pltpu.CompilerParams(
                collective_id=0, has_side_effects=True, vmem_limit_bytes=60 * 2**20
            ),
            name="bed_step",
        )(pos, vel, wts, counts, loff.T, lmask.T, bbox.T, bcell, fluid)
    return tuple(pl.pallas_call(
        write_out,
        out_shape=out_shape,
        in_specs=[vmem] * 3,
        out_specs=(anywhere,) * 3,
        scratch_shapes=[dma((3,))],
        name="out_write",
    )(*results))


def solution(mesh):
    sizes = tuple(mesh.shape[a] for a in ("gx", "gy", "gz"))
    bins = ("gx", "gy", "gz")
    in_specs = (
        P(None, bins, None),
        P(None, bins, None),
        P(bins, None),
        P(bins),
        P(bins, None),
        P(bins, None),
        P(bins, None),
        P(bins),
        P(None, "gx", "gy", "gz"),
    )
    out_specs = (P(None, bins, None), P(None, bins, None), P(None, "gx", "gy", "gz"))
    return jax.shard_map(
        functools.partial(local, sizes),
        mesh=mesh,
        in_specs=in_specs,
        out_specs=out_specs,
        check_vma=False,
    )
```

```python
import functools

import jax
import jax.numpy as jnp
from jax import lax
from jax.experimental import pallas as pl
from jax.experimental.pallas import tpu as pltpu
from jax.sharding import PartitionSpec as P

f32, bf16, i32 = jnp.float32, jnp.bfloat16, jnp.int32
MESH = pl.DeviceIdType.MESH
BINS = 16
STEP, STIFF, DAMP, COUPLING, VISC = 0.1, 0.05, 0.05, 0.004, 0.12
ROOT_LOG2E = 1.4426950408889634**0.5


def iota(shape, dim):
    return lax.broadcasted_iota(i32, shape, dim)


def parts(x):
    high = x.astype(bf16).astype(f32)
    rest = x - high
    middle = rest.astype(bf16).astype(f32)
    return high, middle, rest - middle


def stacked(x):
    return jnp.concatenate([p.astype(bf16) for p in parts(x)], axis=0)


def kernel(
    sizes,
    pos_in,
    vel_in,
    wts_in,
    counts_in,
    loff_in,
    lmask_in,
    bbox_in,
    bcell_in,
    fluid_in,
    pos_out,
    vel_out,
    fluid_out,
    pos,
    vel,
    wts,
    counts,
    loff,
    lmask,
    bbox,
    bcell,
    fluid,
    wide1,
    wide2,
    own_aug,
    aug,
    vals,
    sums,
    pairs,
    req,
    answer,
    ans,
    dep,
    lane_hot,
    row_hot,
    rate_buf,
    first_buf,
    hx,
    hy,
    hz,
    sy,
    sz,
    load_sem,
    halo_send,
    halo_recv,
    group_send,
    group_recv,
    face_send,
    face_recv,
):
    ngx, ngy, ngz = sizes
    group, devices = ngx * ngy, ngx * ngy * ngz
    tiles = -(-group * BINS // 128)
    per_tile = 128 // BINS
    gx, gy, gz = (lax.axis_index(a) for a in ("gx", "gy", "gz"))
    me = gx * ngy + gy
    here = me * ngz + gz

    def in_group(g):
        return (lax.div(g, ngy), lax.rem(g, ngy), gz)

    def at(n):
        g = lax.div(n, ngz)
        return (lax.div(g, ngy), lax.rem(g, ngy), lax.rem(n, ngz))

    bin_right, bin_left = at(lax.rem(here + 1, devices)), at(lax.rem(here + devices - 1, devices))
    faces = (
        (lax.rem(gx + 1, ngx), gy, gz),
        (lax.rem(gx + ngx - 1, ngx), gy, gz),
        (gx, lax.rem(gy + 1, ngy), gz),
        (gx, lax.rem(gy + ngy - 1, ngy), gz),
        (gx, gy, lax.rem(gz + 1, ngz)),
        (gx, gy, lax.rem(gz + ngz - 1, ngz)),
    )

    barrier = pltpu.get_barrier_semaphore()

    @pl.loop(1, group)
    def _(k):
        pl.semaphore_signal(
            barrier, inc=1, device_id=in_group(lax.rem(me + k, group)), device_id_type=MESH
        )

    for other in (bin_right, bin_left, faces[4], faces[5]):
        pl.semaphore_signal(barrier, inc=1, device_id=other, device_id_type=MESH)

    loads = [
        pltpu.make_async_copy(src, dst, load_sem.at[n])
        for n, (src, dst) in enumerate(
            (
                (bbox_in, bbox),
                (bcell_in, bcell),
                (fluid_in, fluid),
                (pos_in, pos),
                (vel_in, vel),
                (counts_in, counts),
                (wts_in, wts),
                (loff_in, loff),
                (lmask_in, lmask),
            )
        )
    ]
    for copy in loads:
        copy.start()

    row8, lane8 = iota((8, 128), 0), iota((8, 128), 1)
    row16, lane16 = iota((16, 128), 0), iota((16, 128), 1)

    loads[0].wait()
    loads[1].wait()
    asked = jnp.zeros((8, 128), i32)
    first_lane = lax.rem(me, per_tile) * BINS
    for b in range(BINS):
        asked = jnp.where(
            lane8 == first_lane + b,
            jnp.where(row8 == 0, bbox[0, b], jnp.where(row8 == 1, bcell[b], 0)),
            asked,
        )
    req[me] = asked

    def face_sources(turn, field):
        for side, (edge_row, edge_lane) in enumerate(((7, 127), (0, 0))):
            rows, lanes = jnp.zeros((16, 128), f32), jnp.zeros((8, 128), f32)
            for c in range(3):
                for x in range(4):
                    k = c * 4 + x
                    tile = field[c, x]
                    rows = jnp.where(row16 == k, tile[edge_row : edge_row + 1, :], rows)
                    lanes = jnp.where(lane8 == k, tile[:, edge_lane : edge_lane + 1], lanes)
            sy[turn, side] = rows
            sz[turn, side] = lanes

    def face_copies(turn, field):
        pairs = (
            (field.at[:, 3], hx.at[turn, 0]),
            (field.at[:, 0], hx.at[turn, 1]),
            (sy.at[turn, 0], hy.at[turn, 0]),
            (sy.at[turn, 1], hy.at[turn, 1]),
            (sz.at[turn, 0], hz.at[turn, 0]),
            (sz.at[turn, 1], hz.at[turn, 1]),
        )
        return [
            pltpu.make_async_remote_copy(
                src_ref=src,
                dst_ref=dst,
                send_sem=face_send.at[turn, n],
                recv_sem=face_recv.at[turn, n],
                device_id=faces[n],
                device_id_type=MESH,
            )
            for n, (src, dst) in enumerate(pairs)
        ]

    def halo_copies(turn, wide):
        own = wide.at[pl.ds(BINS, BINS)]
        return [
            pltpu.make_async_remote_copy(
                src_ref=own,
                dst_ref=wide.at[pl.ds(start, BINS)],
                send_sem=halo_send.at[turn, n],
                recv_sem=halo_recv.at[turn, n],
                device_id=other,
                device_id_type=MESH,
            )
            for n, (start, other) in enumerate(((0, bin_right), (2 * BINS, bin_left)))
        ]

    def group_copy(turn, src, dst, other):
        return pltpu.make_async_remote_copy(
            src_ref=src,
            dst_ref=dst,
            send_sem=group_send.at[turn],
            recv_sem=group_recv.at[turn],
            device_id=other,
            device_id_type=MESH,
        )

    def group_start(turn, buffer, source):
        @pl.loop(1, group)
        def _(k):
            other = lax.rem(me + k, group)
            group_copy(turn, source(other), buffer.at[me], in_group(other)).start()

    def group_all(turn, buffer):
        most = buffer.at[pl.ds(0, group - 1)]
        return group_copy(turn, most, most, in_group(lax.rem(me + 1, group)))

    def gathered(buffer):
        out = []
        for t in range(tiles):
            total = buffer[t * per_tile]
            for s in range(t * per_tile + 1, min(group, (t + 1) * per_tile)):
                total = total + buffer[s]
            out.append(total)
        return jnp.concatenate(out, axis=1) if tiles > 1 else out[0]

    loads[2].wait()
    face_sources(0, fluid)

    for copy in loads[3:]:
        copy.wait()
    for c in range(3):
        wide1[BINS : 2 * BINS, c, :] = pos[c]
        wide1[BINS : 2 * BINS, 3 + c, :] = vel[c]
    count_rows = jnp.zeros((16, 128), i32)
    for b in range(BINS):
        count_rows = jnp.where(row16 == b, counts[b], count_rows)
    occupied = jnp.where(lane16 < count_rows, 1.0, 0.0).astype(f32)
    wide1[BINS : 2 * BINS, 6, :] = wts[...] * occupied
    wide1[BINS : 2 * BINS, 7, :] = occupied

    pl.semaphore_wait(barrier, group - 1 + 4)

    group_start(0, req, lambda other: req.at[me])
    halo1 = halo_copies(0, wide1)
    for copy in halo1:
        copy.start()
    faces0 = face_copies(0, fluid)
    for copy in faces0:
        copy.start()

    def prepare(wide, slot, scale, own):
        tile = wide[slot]
        carried = tile[6:7, :] * scale
        v = jnp.where(row8 < 6, tile, jnp.where(row8 == 6, 1.0, 0.0)) * carried
        vh, vm, vl = parts(v)
        vals[slot] = jnp.concatenate([vh, vm, vl, jnp.zeros_like(vh)], axis=0).astype(bf16)
        y = jnp.where(row8 < 3, tile * ROOT_LOG2E, 0.0)
        norm = -0.5 * jnp.sum(y * y, axis=0, keepdims=True)
        h, m, l = parts(jnp.where(row8 == 3, norm, y))
        ones = jnp.where((row8 >= 4) & (row8 < 7), 1.0, h)
        aug[slot] = jnp.concatenate([ones, m, l, h, m, h], axis=0).astype(bf16)
        if own:
            high = jnp.where(row8 < 3, h, jnp.where(row8 == 3, 1.0, 0.0))
            low = jnp.where(row8 < 3, m, 0.0)
            lowest = jnp.where(row8 < 3, l, 0.0)
            norms = jnp.where(
                row8 == 4,
                h[3:4, :],
                jnp.where(row8 == 5, m[3:4, :], jnp.where(row8 == 6, l[3:4, :], high)),
            )
            own_aug[slot - BINS] = jnp.concatenate(
                [norms, high, high, low, low, lowest], axis=0
            ).astype(bf16)

    def prepare_own(wide):
        @pl.loop(BINS, 2 * BINS, unroll=8)
        def _(slot):
            prepare(wide, slot, 1.0, True)

    has_left = jnp.where(here > 0, 1.0, 0.0).astype(f32)
    has_right = jnp.where(here < devices - 1, 1.0, 0.0).astype(f32)

    def prepare_halo(wide):
        @pl.loop(0, BINS, unroll=4)
        def _(slot):
            prepare(wide, slot, has_left, False)
            prepare(wide, slot + 2 * BINS, has_right, False)

    def near_of(b):
        slots = [b + BINS]
        for q in range(3):
            slots.append(jnp.where(lmask[q, b] != 0, b + BINS + loff[q, b], 3 * BINS))
        return slots

    def contact():
        @pl.loop(0, BINS, unroll=16)
        def _(b):
            near = jnp.concatenate([aug[s] for s in near_of(b)], axis=1)
            exponent = lax.dot_general(
                near, own_aug[b], (((0,), (0,)), ((), ())), preferred_element_type=f32
            )
            pair = jnp.exp2(exponent)
            high = pair.astype(bf16)
            pairs[b, 0:512] = high
            pairs[b, 512:1024] = (pair - high.astype(f32)).astype(bf16)

        @pl.loop(0, BINS, unroll=16)
        def _(b):
            value = jnp.concatenate([vals[s] for s in near_of(b)], axis=1)
            total = jnp.dot(value, pairs[b, 0:512], preferred_element_type=f32)
            total = total + jnp.dot(value, pairs[b, 512:1024], preferred_element_type=f32)
            sums[b] = total[0:8] + total[8:16] + total[16:24]

    def pushed_by(tile, total):
        net = tile * total[6:7, :] - total
        return STIFF * pltpu.roll(net, 3, 0) - DAMP * net

    def advanced(tile, force, seen):
        held = STEP * tile[7:8, :]
        new_v = tile + held * (force + (seen - tile))
        new_x = tile + held * pltpu.roll(new_v, 5, 0)
        return jnp.where(row8 < 3, new_x, jnp.where(row8 < 6, new_v, tile))

    aug[3 * BINS] = jnp.zeros((48, 128), bf16)
    vals[3 * BINS] = jnp.zeros((32, 128), bf16)
    prepare_own(wide1)

    group_all(0, req).wait_recv()
    asked_all = gathered(req)
    wide_lanes = 128 * tiles
    cell = asked_all[1:2, :]
    lane_hot[...] = jnp.where(
        iota((128, wide_lanes), 0) == (cell & 127), 1.0, 0.0
    ).astype(bf16)
    row_hot[...] = jnp.where(
        (iota((32, wide_lanes), 0) == (cell >> 7)) & (asked_all[0:1, :] == me), 1.0, 0.0
    ).astype(f32)
    at_lane = jnp.dot(
        stacked(fluid[...].reshape(96, 128)), lane_hot[...], preferred_element_type=f32
    )
    at_lane = at_lane[0:96] + at_lane[96:192] + at_lane[192:288]
    reply = jnp.zeros((8, wide_lanes), f32)
    wide_row = iota((8, wide_lanes), 0)
    for c in range(3):
        picked = jnp.sum(at_lane[32 * c : 32 * c + 32] * row_hot[...], axis=0, keepdims=True)
        reply = jnp.where(wide_row == 3 + c, picked, reply)
    for t in range(tiles):
        answer[t] = reply[:, 128 * t : 128 * t + 128]
    ans[me] = answer[lax.div(me, per_tile)]
    group_start(1, ans, lambda other: answer.at[lax.div(other, per_tile)])

    in_x = [jnp.where(g, 1.0, 0.0).astype(f32) for g in (gx > 0, gx < ngx - 1)]
    in_y = [jnp.where(g, 1.0, 0.0).astype(f32) for g in (gy > 0, gy < ngy - 1)]
    in_z = [jnp.where(g, 1.0, 0.0).astype(f32) for g in (gz > 0, gz < ngz - 1)]

    def laplace(turn, field, c, x):
        k = c * 4 + x
        tile = field[c, x]
        below = field[c, x - 1] if x > 0 else hx[turn, 0, c] * in_x[0]
        above = field[c, x + 1] if x < 3 else hx[turn, 1, c] * in_x[1]
        total = below + above - 6.0 * tile
        total = total + jnp.where(
            row8 == 0, hy[turn, 0, k : k + 1, :] * in_y[0], pltpu.roll(tile, 1, 0)
        )
        total = total + jnp.where(
            row8 == 7, hy[turn, 1, k : k + 1, :] * in_y[1], pltpu.roll(tile, 7, 0)
        )
        zl, zr = hz[turn, 0] * in_z[0], hz[turn, 1] * in_z[1]
        total = total + jnp.where(lane8 == 0, zl[:, k : k + 1], pltpu.roll(tile, 1, 1))
        return total + jnp.where(lane8 == 127, zr[:, k : k + 1], pltpu.roll(tile, 127, 1))

    for copy in faces0:
        copy.wait_recv()
    for c in range(3):
        for x in range(4):
            rate_buf[c, x] = VISC * laplace(0, fluid, c, x)

    for copy in halo1:
        copy.wait_recv()
    prepare_halo(wide1)

    contact()

    drawn = jnp.zeros((8, 128), f32)
    for b in range(BINS):
        tile = wide1[BINS + b]
        force = pushed_by(tile, sums[b])
        held = STEP * tile[7:8, :]
        term = jnp.where(row8 == 6, 2.0 - held, held * (tile - force) - 2.0 * tile)
        drawn = jnp.where(
            lane8 == b, jnp.sum(tile[6:7, :] * term, axis=1, keepdims=True), drawn
        )
        sums[b] = force
    dep[me] = pltpu.roll(drawn, first_lane, 1)
    group_start(2, dep, lambda other: dep.at[me])

    group_all(1, ans).wait_recv()
    seen = ans[0]
    for s in range(1, group):
        seen = seen + ans[s]
    seen = pltpu.roll(seen, lax.rem(128 - first_lane, 128), 1)
    for b in range(BINS):
        seen_b = jnp.broadcast_to(seen[:, b : b + 1], (8, 128))
        wide2[BINS + b] = advanced(wide1[BINS + b], sums[b], seen_b)
    halo2 = halo_copies(1, wide2)
    for copy in halo2:
        copy.start()
    prepare_own(wide2)

    group_all(2, dep).wait_recv()
    drawn_all = gathered(dep)
    there = [answer[t] for t in range(tiles)]
    there = jnp.concatenate(there, axis=1) if tiles > 1 else there[0]
    pushed = -COUPLING * (drawn_all[6:7, :] * there + drawn_all)
    spread = jnp.concatenate(
        [pushed[3 + c : 4 + c, :] * row_hot[...] for c in range(3)], axis=0
    )
    source = lax.dot_general(
        stacked(spread), lane_hot[...], (((1,), (1,)), ((), ())), preferred_element_type=f32
    )
    source = source[0:96] + source[96:192] + source[192:288]
    first_buf[...] = rate_buf[...] + source.reshape(3, 4, 8, 128)
    face_sources(1, first_buf)
    faces1 = face_copies(1, first_buf)
    for copy in faces1:
        copy.start()

    for copy in halo2:
        copy.wait_recv()
    prepare_halo(wide2)

    contact()

    for b in range(BINS):
        tile, seen_b = wide2[BINS + b], jnp.broadcast_to(seen[:, b : b + 1], (8, 128))
        sums[b] = advanced(tile, pushed_by(tile, sums[b]), seen_b)
    for c in range(3):
        pos_out[c] = sums[:, c, :]
        vel_out[c] = sums[:, 3 + c, :]

    for copy in faces1:
        copy.wait_recv()
    for c in range(3):
        for x in range(4):
            fluid_out[c, x] = (
                fluid[c, x] + first_buf[c, x] + (0.5 * VISC) * laplace(1, first_buf, c, x)
            )

    for copy in (*halo1, *faces0, *halo2, *faces1):
        copy.wait_send()
    for turn, buffer in enumerate((req, ans, dep)):
        group_all(turn, buffer).wait_send()


def write_out(*refs):
    sems = refs[-1]
    copies = [pltpu.make_async_copy(refs[n], refs[3 + n], sems.at[n]) for n in range(3)]
    for copy in copies:
        copy.start()
    for copy in copies:
        copy.wait()


def local(sizes, pos, vel, wts, counts, loff, lmask, bbox, bcell, fluid):
    group = sizes[0] * sizes[1]
    tiles = -(-group * BINS // 128)
    vmem, anywhere = pl.BlockSpec(memory_space=pltpu.VMEM), pl.BlockSpec(memory_space=pltpu.HBM)
    dma = pltpu.SemaphoreType.DMA
    out_shape = (
        jax.ShapeDtypeStruct((3, BINS, 128), f32),
        jax.ShapeDtypeStruct((3, BINS, 128), f32),
        jax.ShapeDtypeStruct((3, 4, 8, 128), f32),
    )
    results = pl.pallas_call(
            functools.partial(kernel, sizes),
            out_shape=out_shape,
            in_specs=[anywhere] * 9,
            out_specs=(vmem,) * 3,
            scratch_shapes=[
                pltpu.VMEM((3, BINS, 128), f32),
                pltpu.VMEM((3, BINS, 128), f32),
                pltpu.VMEM((BINS, 128), f32),
                pltpu.SMEM((BINS,), i32),
                pltpu.SMEM((3, BINS), i32),
                pltpu.SMEM((3, BINS), i32),
                pltpu.SMEM((1, BINS), i32),
                pltpu.SMEM((BINS,), i32),
                pltpu.VMEM((3, 4, 8, 128), f32),
                pltpu.VMEM((3 * BINS, 8, 128), f32),
                pltpu.VMEM((3 * BINS, 8, 128), f32),
                pltpu.VMEM((BINS, 48, 128), bf16),
                pltpu.VMEM((3 * BINS + 1, 48, 128), bf16),
                pltpu.VMEM((3 * BINS + 1, 32, 128), bf16),
                pltpu.VMEM((BINS, 8, 128), f32),
                pltpu.VMEM((BINS, 1024, 128), bf16),
                pltpu.VMEM((group, 8, 128), i32),
                pltpu.VMEM((tiles, 8, 128), f32),
                pltpu.VMEM((group, 8, 128), f32),
                pltpu.VMEM((group, 8, 128), f32),
                pltpu.VMEM((128, 128 * tiles), bf16),
                pltpu.VMEM((32, 128 * tiles), f32),
                pltpu.VMEM((3, 4, 8, 128), f32),
                pltpu.VMEM((3, 4, 8, 128), f32),
                pltpu.VMEM((2, 2, 3, 8, 128), f32),
                pltpu.VMEM((2, 2, 16, 128), f32),
                pltpu.VMEM((2, 2, 8, 128), f32),
                pltpu.VMEM((2, 2, 16, 128), f32),
                pltpu.VMEM((2, 2, 8, 128), f32),
                dma((9,)),
                dma((2, 2)),
                dma((2, 2)),
                dma((3,)),
                dma((3,)),
                dma((2, 6)),
                dma((2, 6)),
            ],
            compiler_params=pltpu.CompilerParams(
                collective_id=0, has_side_effects=True, vmem_limit_bytes=60 * 2**20
            ),
            name="bed_step",
        )(pos, vel, wts, counts, loff.T, lmask.T, bbox.T, bcell, fluid)
    return tuple(pl.pallas_call(
        write_out,
        out_shape=out_shape,
        in_specs=[vmem] * 3,
        out_specs=(anywhere,) * 3,
        scratch_shapes=[dma((3,))],
        name="out_write",
    )(*results))


def solution(mesh):
    sizes = tuple(mesh.shape[a] for a in ("gx", "gy", "gz"))
    bins = ("gx", "gy", "gz")
    in_specs = (
        P(None, bins, None),
        P(None, bins, None),
        P(bins, None),
        P(bins),
        P(bins, None),
        P(bins, None),
        P(bins, None),
        P(bins),
        P(None, "gx", "gy", "gz"),
    )
    out_specs = (P(None, bins, None), P(None, bins, None), P(None, "gx", "gy", "gz"))
    return jax.shard_map(
        functools.partial(local, sizes),
        mesh=mesh,
        in_specs=in_specs,
        out_specs=out_specs,
        check_vma=False,
    )
```

```python
import functools

import jax
import jax.numpy as jnp
from jax import lax
from jax.experimental import pallas as pl
from jax.experimental.pallas import tpu as pltpu
from jax.sharding import PartitionSpec as P

f32, bf16, i32 = jnp.float32, jnp.bfloat16, jnp.int32
MESH = pl.DeviceIdType.MESH
BINS = 16
STEP, STIFF, DAMP, COUPLING, VISC = 0.1, 0.05, 0.05, 0.004, 0.12
ROOT_LOG2E = 1.4426950408889634**0.5


def iota(shape, dim):
    return lax.broadcasted_iota(i32, shape, dim)


def parts(x):
    high = x.astype(bf16).astype(f32)
    rest = x - high
    middle = rest.astype(bf16).astype(f32)
    return high, middle, rest - middle


def stacked(x):
    return jnp.concatenate([p.astype(bf16) for p in parts(x)], axis=0)


def kernel(
    sizes,
    pos_in,
    vel_in,
    wts_in,
    counts_in,
    loff_in,
    lmask_in,
    bbox_in,
    bcell_in,
    fluid_in,
    pos_out,
    vel_out,
    fluid_out,
    pos,
    vel,
    wts,
    counts,
    loff,
    lmask,
    bbox,
    bcell,
    fluid,
    wide1,
    wide2,
    own_aug,
    aug,
    vals,
    sums,
    pairs,
    req,
    answer,
    ans,
    dep,
    lane_hot,
    row_hot,
    rate_buf,
    first_buf,
    hx,
    hy,
    hz,
    sy,
    sz,
    load_sem,
    halo_send,
    halo_recv,
    group_send,
    group_recv,
    face_send,
    face_recv,
):
    ngx, ngy, ngz = sizes
    group, devices = ngx * ngy, ngx * ngy * ngz
    tiles = -(-group * BINS // 128)
    per_tile = 128 // BINS
    gx, gy, gz = (lax.axis_index(a) for a in ("gx", "gy", "gz"))
    me = gx * ngy + gy
    here = me * ngz + gz

    def in_group(g):
        return (lax.div(g, ngy), lax.rem(g, ngy), gz)

    def at(n):
        g = lax.div(n, ngz)
        return (lax.div(g, ngy), lax.rem(g, ngy), lax.rem(n, ngz))

    bin_right, bin_left = at(lax.rem(here + 1, devices)), at(lax.rem(here + devices - 1, devices))
    faces = (
        (lax.rem(gx + 1, ngx), gy, gz),
        (lax.rem(gx + ngx - 1, ngx), gy, gz),
        (gx, lax.rem(gy + 1, ngy), gz),
        (gx, lax.rem(gy + ngy - 1, ngy), gz),
        (gx, gy, lax.rem(gz + 1, ngz)),
        (gx, gy, lax.rem(gz + ngz - 1, ngz)),
    )

    barrier = pltpu.get_barrier_semaphore()

    for other in (bin_right, bin_left, faces[4], faces[5]):
        pl.semaphore_signal(barrier, inc=1, device_id=other, device_id_type=MESH)

    @pl.loop(1, group)
    def _(k):
        pl.semaphore_signal(
            barrier, inc=1, device_id=in_group(lax.rem(me + k, group)), device_id_type=MESH
        )

    loads = [
        pltpu.make_async_copy(src, dst, load_sem.at[n])
        for n, (src, dst) in enumerate(
            (
                (bbox_in, bbox),
                (bcell_in, bcell),
                (fluid_in, fluid),
                (pos_in, pos),
                (vel_in, vel),
                (counts_in, counts),
                (wts_in, wts),
                (loff_in, loff),
                (lmask_in, lmask),
            )
        )
    ]
    for copy in loads:
        copy.start()

    row8, lane8 = iota((8, 128), 0), iota((8, 128), 1)
    row16, lane16 = iota((16, 128), 0), iota((16, 128), 1)

    loads[0].wait()
    loads[1].wait()
    asked = jnp.zeros((8, 128), i32)
    first_lane = lax.rem(me, per_tile) * BINS
    for b in range(BINS):
        asked = jnp.where(
            lane8 == first_lane + b,
            jnp.where(row8 == 0, bbox[0, b], jnp.where(row8 == 1, bcell[b], 0)),
            asked,
        )
    req[me] = asked

    def face_sources(turn, field):
        for side, (edge_row, edge_lane) in enumerate(((7, 127), (0, 0))):
            rows, lanes = jnp.zeros((16, 128), f32), jnp.zeros((8, 128), f32)
            for c in range(3):
                for x in range(4):
                    k = c * 4 + x
                    tile = field[c, x]
                    rows = jnp.where(row16 == k, tile[edge_row : edge_row + 1, :], rows)
                    lanes = jnp.where(lane8 == k, tile[:, edge_lane : edge_lane + 1], lanes)
            sy[turn, side] = rows
            sz[turn, side] = lanes

    def face_copies(turn, field):
        pairs = (
            (field.at[:, 3], hx.at[turn, 0]),
            (field.at[:, 0], hx.at[turn, 1]),
            (sy.at[turn, 0], hy.at[turn, 0]),
            (sy.at[turn, 1], hy.at[turn, 1]),
            (sz.at[turn, 0], hz.at[turn, 0]),
            (sz.at[turn, 1], hz.at[turn, 1]),
        )
        return [
            pltpu.make_async_remote_copy(
                src_ref=src,
                dst_ref=dst,
                send_sem=face_send.at[turn, n],
                recv_sem=face_recv.at[turn, n],
                device_id=faces[n],
                device_id_type=MESH,
            )
            for n, (src, dst) in enumerate(pairs)
        ]

    def halo_copies(turn, wide):
        own = wide.at[pl.ds(BINS, BINS)]
        return [
            pltpu.make_async_remote_copy(
                src_ref=own,
                dst_ref=wide.at[pl.ds(start, BINS)],
                send_sem=halo_send.at[turn, n],
                recv_sem=halo_recv.at[turn, n],
                device_id=other,
                device_id_type=MESH,
            )
            for n, (start, other) in enumerate(((0, bin_right), (2 * BINS, bin_left)))
        ]

    def group_copy(turn, src, dst, other):
        return pltpu.make_async_remote_copy(
            src_ref=src,
            dst_ref=dst,
            send_sem=group_send.at[turn],
            recv_sem=group_recv.at[turn],
            device_id=other,
            device_id_type=MESH,
        )

    def group_start(turn, buffer, source):
        @pl.loop(1, group)
        def _(k):
            other = lax.rem(me + k, group)
            group_copy(turn, source(other), buffer.at[me], in_group(other)).start()

    def group_all(turn, buffer):
        most = buffer.at[pl.ds(0, group - 1)]
        return group_copy(turn, most, most, in_group(lax.rem(me + 1, group)))

    def gathered(buffer):
        out = []
        for t in range(tiles):
            total = buffer[t * per_tile]
            for s in range(t * per_tile + 1, min(group, (t + 1) * per_tile)):
                total = total + buffer[s]
            out.append(total)
        return jnp.concatenate(out, axis=1) if tiles > 1 else out[0]

    loads[2].wait()
    face_sources(0, fluid)

    for copy in loads[3:]:
        copy.wait()
    for c in range(3):
        wide1[BINS : 2 * BINS, c, :] = pos[c]
        wide1[BINS : 2 * BINS, 3 + c, :] = vel[c]
    count_rows = jnp.zeros((16, 128), i32)
    for b in range(BINS):
        count_rows = jnp.where(row16 == b, counts[b], count_rows)
    occupied = jnp.where(lane16 < count_rows, 1.0, 0.0).astype(f32)
    wide1[BINS : 2 * BINS, 6, :] = wts[...] * occupied
    wide1[BINS : 2 * BINS, 7, :] = occupied

    pl.semaphore_wait(barrier, group - 1 + 4)

    halo1 = halo_copies(0, wide1)
    for copy in halo1:
        copy.start()
    group_start(0, req, lambda other: req.at[me])
    faces0 = face_copies(0, fluid)
    for copy in faces0:
        copy.start()

    def prepare(wide, slot, scale, own):
        tile = wide[slot]
        carried = tile[6:7, :] * scale
        v = jnp.where(row8 < 6, tile, jnp.where(row8 == 6, 1.0, 0.0)) * carried
        vh, vm, vl = parts(v)
        vals[slot] = jnp.concatenate([vh, vm, vl, jnp.zeros_like(vh)], axis=0).astype(bf16)
        y = jnp.where(row8 < 3, tile * ROOT_LOG2E, 0.0)
        norm = -0.5 * jnp.sum(y * y, axis=0, keepdims=True)
        h, m, l = parts(jnp.where(row8 == 3, norm, y))
        ones = jnp.where((row8 >= 4) & (row8 < 7), 1.0, h)
        aug[slot] = jnp.concatenate([ones, m, l, h, m, h], axis=0).astype(bf16)
        if own:
            high = jnp.where(row8 < 3, h, jnp.where(row8 == 3, 1.0, 0.0))
            low = jnp.where(row8 < 3, m, 0.0)
            lowest = jnp.where(row8 < 3, l, 0.0)
            norms = jnp.where(
                row8 == 4,
                h[3:4, :],
                jnp.where(row8 == 5, m[3:4, :], jnp.where(row8 == 6, l[3:4, :], high)),
            )
            own_aug[slot - BINS] = jnp.concatenate(
                [norms, high, high, low, low, lowest], axis=0
            ).astype(bf16)

    def prepare_own(wide):
        @pl.loop(BINS, 2 * BINS, unroll=8)
        def _(slot):
            prepare(wide, slot, 1.0, True)

    has_left = jnp.where(here > 0, 1.0, 0.0).astype(f32)
    has_right = jnp.where(here < devices - 1, 1.0, 0.0).astype(f32)

    def prepare_halo(wide):
        @pl.loop(0, BINS, unroll=4)
        def _(slot):
            prepare(wide, slot, has_left, False)
            prepare(wide, slot + 2 * BINS, has_right, False)

    def near_of(b):
        slots = [b + BINS]
        for q in range(3):
            slots.append(jnp.where(lmask[q, b] != 0, b + BINS + loff[q, b], 3 * BINS))
        return slots

    def pair_kernel(b, slots, first):
        near = jnp.concatenate([aug[s] for s in slots], axis=1)
        exponent = lax.dot_general(
            near, own_aug[b], (((0,), (0,)), ((), ())), preferred_element_type=f32
        )
        pair = jnp.exp2(exponent)
        high = pair.astype(bf16)
        size = 128 * len(slots)
        pairs[b, first : first + size] = high
        pairs[b, 512 + first : 512 + first + size] = (pair - high.astype(f32)).astype(bf16)

    def contact_own():
        @pl.loop(0, BINS, unroll=16)
        def _(b):
            pair_kernel(b, [b + BINS], 0)

    def contact():
        @pl.loop(0, BINS, unroll=16)
        def _(b):
            pair_kernel(b, near_of(b)[1:], 128)

        @pl.loop(0, BINS, unroll=16)
        def _(b):
            value = jnp.concatenate([vals[s] for s in near_of(b)], axis=1)
            total = jnp.dot(value, pairs[b, 0:512], preferred_element_type=f32)
            total = total + jnp.dot(value, pairs[b, 512:1024], preferred_element_type=f32)
            sums[b] = total[0:8] + total[8:16] + total[16:24]

    def pushed_by(tile, total):
        net = tile * total[6:7, :] - total
        return STIFF * pltpu.roll(net, 3, 0) - DAMP * net

    def advanced(tile, force, seen):
        held = STEP * tile[7:8, :]
        new_v = tile + held * (force + (seen - tile))
        new_x = tile + held * pltpu.roll(new_v, 5, 0)
        return jnp.where(row8 < 3, new_x, jnp.where(row8 < 6, new_v, tile))

    aug[3 * BINS] = jnp.zeros((48, 128), bf16)
    vals[3 * BINS] = jnp.zeros((32, 128), bf16)
    prepare_own(wide1)
    contact_own()

    group_all(0, req).wait_recv()
    asked_all = gathered(req)
    wide_lanes = 128 * tiles
    cell = asked_all[1:2, :]
    lane_hot[...] = jnp.where(
        iota((128, wide_lanes), 0) == (cell & 127), 1.0, 0.0
    ).astype(bf16)
    row_hot[...] = jnp.where(
        (iota((32, wide_lanes), 0) == (cell >> 7)) & (asked_all[0:1, :] == me), 1.0, 0.0
    ).astype(f32)
    at_lane = jnp.dot(
        stacked(fluid[...].reshape(96, 128)), lane_hot[...], preferred_element_type=f32
    )
    at_lane = at_lane[0:96] + at_lane[96:192] + at_lane[192:288]
    reply = jnp.zeros((8, wide_lanes), f32)
    wide_row = iota((8, wide_lanes), 0)
    for c in range(3):
        picked = jnp.sum(at_lane[32 * c : 32 * c + 32] * row_hot[...], axis=0, keepdims=True)
        reply = jnp.where(wide_row == 3 + c, picked, reply)
    for t in range(tiles):
        answer[t] = reply[:, 128 * t : 128 * t + 128]
    ans[me] = answer[lax.div(me, per_tile)]
    group_start(1, ans, lambda other: answer.at[lax.div(other, per_tile)])

    in_x = [jnp.where(g, 1.0, 0.0).astype(f32) for g in (gx > 0, gx < ngx - 1)]
    in_y = [jnp.where(g, 1.0, 0.0).astype(f32) for g in (gy > 0, gy < ngy - 1)]
    in_z = [jnp.where(g, 1.0, 0.0).astype(f32) for g in (gz > 0, gz < ngz - 1)]

    def laplace(turn, field, c, x):
        k = c * 4 + x
        tile = field[c, x]
        below = field[c, x - 1] if x > 0 else hx[turn, 0, c] * in_x[0]
        above = field[c, x + 1] if x < 3 else hx[turn, 1, c] * in_x[1]
        total = below + above - 6.0 * tile
        total = total + jnp.where(
            row8 == 0, hy[turn, 0, k : k + 1, :] * in_y[0], pltpu.roll(tile, 1, 0)
        )
        total = total + jnp.where(
            row8 == 7, hy[turn, 1, k : k + 1, :] * in_y[1], pltpu.roll(tile, 7, 0)
        )
        zl, zr = hz[turn, 0] * in_z[0], hz[turn, 1] * in_z[1]
        total = total + jnp.where(lane8 == 0, zl[:, k : k + 1], pltpu.roll(tile, 1, 1))
        return total + jnp.where(lane8 == 127, zr[:, k : k + 1], pltpu.roll(tile, 127, 1))

    for copy in halo1:
        copy.wait_recv()
    prepare_halo(wide1)

    contact()

    drawn = jnp.zeros((8, 128), f32)
    for b in range(BINS):
        tile = wide1[BINS + b]
        force = pushed_by(tile, sums[b])
        held = STEP * tile[7:8, :]
        term = jnp.where(row8 == 6, 2.0 - held, held * (tile - force) - 2.0 * tile)
        drawn = jnp.where(
            lane8 == b, jnp.sum(tile[6:7, :] * term, axis=1, keepdims=True), drawn
        )
        sums[b] = force
    dep[me] = pltpu.roll(drawn, first_lane, 1)
    group_start(2, dep, lambda other: dep.at[me])

    for copy in faces0:
        copy.wait_recv()
    for c in range(3):
        for x in range(4):
            rate_buf[c, x] = VISC * laplace(0, fluid, c, x)

    group_all(1, ans).wait_recv()
    seen = ans[0]
    for s in range(1, group):
        seen = seen + ans[s]
    seen = pltpu.roll(seen, lax.rem(128 - first_lane, 128), 1)
    for b in range(BINS):
        seen_b = jnp.broadcast_to(seen[:, b : b + 1], (8, 128))
        wide2[BINS + b] = advanced(wide1[BINS + b], sums[b], seen_b)
    halo2 = halo_copies(1, wide2)
    for copy in halo2:
        copy.start()
    prepare_own(wide2)
    contact_own()

    group_all(2, dep).wait_recv()
    drawn_all = gathered(dep)
    there = [answer[t] for t in range(tiles)]
    there = jnp.concatenate(there, axis=1) if tiles > 1 else there[0]
    pushed = -COUPLING * (drawn_all[6:7, :] * there + drawn_all)
    spread = jnp.concatenate(
        [pushed[3 + c : 4 + c, :] * row_hot[...] for c in range(3)], axis=0
    )
    source = lax.dot_general(
        stacked(spread), lane_hot[...], (((1,), (1,)), ((), ())), preferred_element_type=f32
    )
    source = source[0:96] + source[96:192] + source[192:288]
    first_buf[...] = rate_buf[...] + source.reshape(3, 4, 8, 128)
    face_sources(1, first_buf)
    faces1 = face_copies(1, first_buf)
    for copy in faces1:
        copy.start()

    for copy in halo2:
        copy.wait_recv()
    prepare_halo(wide2)

    contact()

    for b in range(BINS):
        tile, seen_b = wide2[BINS + b], jnp.broadcast_to(seen[:, b : b + 1], (8, 128))
        sums[b] = advanced(tile, pushed_by(tile, sums[b]), seen_b)
    for c in range(3):
        pos_out[c] = sums[:, c, :]
        vel_out[c] = sums[:, 3 + c, :]

    for copy in faces1:
        copy.wait_recv()
    for c in range(3):
        for x in range(4):
            fluid_out[c, x] = (
                fluid[c, x] + first_buf[c, x] + (0.5 * VISC) * laplace(1, first_buf, c, x)
            )

    for copy in (*halo1, *faces0, *halo2, *faces1):
        copy.wait_send()
    for turn, buffer in enumerate((req, ans, dep)):
        group_all(turn, buffer).wait_send()


def write_out(*refs):
    sems = refs[-1]
    copies = [pltpu.make_async_copy(refs[n], refs[3 + n], sems.at[n]) for n in range(3)]
    for copy in copies:
        copy.start()
    for copy in copies:
        copy.wait()


def local(sizes, pos, vel, wts, counts, loff, lmask, bbox, bcell, fluid):
    group = sizes[0] * sizes[1]
    tiles = -(-group * BINS // 128)
    vmem, anywhere = pl.BlockSpec(memory_space=pltpu.VMEM), pl.BlockSpec(memory_space=pltpu.HBM)
    dma = pltpu.SemaphoreType.DMA
    args = (pos, vel, wts, counts, loff.T, lmask.T, bbox.T, bcell, fluid)
    out_shape = (
        jax.ShapeDtypeStruct((3, BINS, 128), f32),
        jax.ShapeDtypeStruct((3, BINS, 128), f32),
        jax.ShapeDtypeStruct((3, 4, 8, 128), f32),
    )
    results = pl.pallas_call(
            functools.partial(kernel, sizes),
            out_shape=out_shape,
            in_specs=[anywhere] * 9,
            out_specs=(vmem,) * 3,
            scratch_shapes=[
                pltpu.VMEM((3, BINS, 128), f32),
                pltpu.VMEM((3, BINS, 128), f32),
                pltpu.VMEM((BINS, 128), f32),
                pltpu.SMEM((BINS,), i32),
                pltpu.SMEM((3, BINS), i32),
                pltpu.SMEM((3, BINS), i32),
                pltpu.SMEM((1, BINS), i32),
                pltpu.SMEM((BINS,), i32),
                pltpu.VMEM((3, 4, 8, 128), f32),
                pltpu.VMEM((3 * BINS, 8, 128), f32),
                pltpu.VMEM((3 * BINS, 8, 128), f32),
                pltpu.VMEM((BINS, 48, 128), bf16),
                pltpu.VMEM((3 * BINS + 1, 48, 128), bf16),
                pltpu.VMEM((3 * BINS + 1, 32, 128), bf16),
                pltpu.VMEM((BINS, 8, 128), f32),
                pltpu.VMEM((BINS, 1024, 128), bf16),
                pltpu.VMEM((group, 8, 128), i32),
                pltpu.VMEM((tiles, 8, 128), f32),
                pltpu.VMEM((group, 8, 128), f32),
                pltpu.VMEM((group, 8, 128), f32),
                pltpu.VMEM((128, 128 * tiles), bf16),
                pltpu.VMEM((32, 128 * tiles), f32),
                pltpu.VMEM((3, 4, 8, 128), f32),
                pltpu.VMEM((3, 4, 8, 128), f32),
                pltpu.VMEM((2, 2, 3, 8, 128), f32),
                pltpu.VMEM((2, 2, 16, 128), f32),
                pltpu.VMEM((2, 2, 8, 128), f32),
                pltpu.VMEM((2, 2, 16, 128), f32),
                pltpu.VMEM((2, 2, 8, 128), f32),
                dma((9,)),
                dma((2, 2)),
                dma((2, 2)),
                dma((3,)),
                dma((3,)),
                dma((2, 6)),
                dma((2, 6)),
            ],
            compiler_params=pltpu.CompilerParams(
                collective_id=0, has_side_effects=True, vmem_limit_bytes=16 * 2**20
            ),
            name="bed_step",
        )(*(pltpu.with_memory_space_constraint(x, pltpu.HBM) for x in args))
    return tuple(pl.pallas_call(
        write_out,
        out_shape=out_shape,
        in_specs=[vmem] * 3,
        out_specs=(anywhere,) * 3,
        scratch_shapes=[dma((3,))],
        compiler_params=pltpu.CompilerParams(vmem_limit_bytes=4 * 2**20),
        name="out_write",
    )(*results))


def solution(mesh):
    sizes = tuple(mesh.shape[a] for a in ("gx", "gy", "gz"))
    bins = ("gx", "gy", "gz")
    in_specs = (
        P(None, bins, None),
        P(None, bins, None),
        P(bins, None),
        P(bins),
        P(bins, None),
        P(bins, None),
        P(bins, None),
        P(bins),
        P(None, "gx", "gy", "gz"),
    )
    out_specs = (P(None, bins, None), P(None, bins, None), P(None, "gx", "gy", "gz"))
    return jax.shard_map(
        functools.partial(local, sizes),
        mesh=mesh,
        in_specs=in_specs,
        out_specs=out_specs,
        check_vma=False,
    )
```

```python
import functools

import jax
import jax.numpy as jnp
from jax import lax
from jax.experimental import pallas as pl
from jax.experimental.pallas import tpu as pltpu
from jax.sharding import PartitionSpec as P

f32, bf16, i32 = jnp.float32, jnp.bfloat16, jnp.int32
MESH = pl.DeviceIdType.MESH
BINS = 16
STEP, STIFF, DAMP, COUPLING, VISC = 0.1, 0.05, 0.05, 0.004, 0.12
ROOT_LOG2E = 1.4426950408889634**0.5


def iota(shape, dim):
    return lax.broadcasted_iota(i32, shape, dim)


def parts(x):
    high = x.astype(bf16).astype(f32)
    rest = x - high
    middle = rest.astype(bf16).astype(f32)
    return high, middle, rest - middle


def stacked(x):
    return jnp.concatenate([p.astype(bf16) for p in parts(x)], axis=0)


def kernel(
    sizes,
    pos_in,
    vel_in,
    wts_in,
    counts_in,
    loff_in,
    lmask_in,
    bbox_in,
    bcell_in,
    fluid_in,
    pos_out,
    vel_out,
    fluid_out,
    pos,
    vel,
    wts,
    counts,
    loff,
    lmask,
    bbox,
    bcell,
    fluid,
    wide1,
    wide2,
    own_aug,
    aug,
    vals,
    sums,
    pairs,
    req,
    answer,
    ans,
    dep,
    lane_hot,
    row_hot,
    fluid_parts,
    rate_buf,
    first_buf,
    hx,
    hy,
    hz,
    sy,
    sz,
    load_sem,
    halo_send,
    halo_recv,
    group_send,
    group_recv,
    face_send,
    face_recv,
):
    ngx, ngy, ngz = sizes
    group, devices = ngx * ngy, ngx * ngy * ngz
    tiles = -(-group * BINS // 128)
    per_tile = 128 // BINS
    gx, gy, gz = (lax.axis_index(a) for a in ("gx", "gy", "gz"))
    me = gx * ngy + gy
    here = me * ngz + gz

    def in_group(g):
        return (lax.div(g, ngy), lax.rem(g, ngy), gz)

    def at(n):
        g = lax.div(n, ngz)
        return (lax.div(g, ngy), lax.rem(g, ngy), lax.rem(n, ngz))

    bin_right, bin_left = at(lax.rem(here + 1, devices)), at(lax.rem(here + devices - 1, devices))
    faces = (
        (lax.rem(gx + 1, ngx), gy, gz),
        (lax.rem(gx + ngx - 1, ngx), gy, gz),
        (gx, lax.rem(gy + 1, ngy), gz),
        (gx, lax.rem(gy + ngy - 1, ngy), gz),
        (gx, gy, lax.rem(gz + 1, ngz)),
        (gx, gy, lax.rem(gz + ngz - 1, ngz)),
    )

    barrier = pltpu.get_barrier_semaphore()

    for other in (bin_right, bin_left, faces[4], faces[5]):
        pl.semaphore_signal(barrier, inc=1, device_id=other, device_id_type=MESH)

    @pl.loop(1, group)
    def _(k):
        pl.semaphore_signal(
            barrier, inc=1, device_id=in_group(lax.rem(me + k, group)), device_id_type=MESH
        )

    loads = [
        pltpu.make_async_copy(src, dst, load_sem.at[n])
        for n, (src, dst) in enumerate(
            (
                (bbox_in, bbox),
                (bcell_in, bcell),
                (fluid_in, fluid),
                (pos_in, pos),
                (vel_in, vel),
                (counts_in, counts),
                (wts_in, wts),
                (loff_in, loff),
                (lmask_in, lmask),
            )
        )
    ]
    for copy in loads:
        copy.start()

    row8, lane8 = iota((8, 128), 0), iota((8, 128), 1)
    row16, lane16 = iota((16, 128), 0), iota((16, 128), 1)

    loads[0].wait()
    loads[1].wait()
    asked = jnp.zeros((8, 128), i32)
    first_lane = lax.rem(me, per_tile) * BINS
    for b in range(BINS):
        asked = jnp.where(
            lane8 == first_lane + b,
            jnp.where(row8 == 0, bbox[0, b], jnp.where(row8 == 1, bcell[b], 0)),
            asked,
        )
    req[me] = asked

    def pack_y(turn, field):
        for side, edge in enumerate((7, 0)):
            rows = jnp.zeros((16, 128), f32)
            for k in range(12):
                rows = jnp.where(row16 == k, field[k // 4, k % 4, edge : edge + 1, :], rows)
            sy[turn, side] = rows

    def pack_z(turn, field):
        for side, edge in enumerate((127, 0)):
            lanes = jnp.zeros((8, 128), f32)
            for k in range(12):
                tile = field[k // 4, k % 4]
                lanes = jnp.where(lane8 == k, tile[:, edge : edge + 1], lanes)
            sz[turn, side] = lanes

    def face_copies(turn, field):
        pairs = (
            (field.at[:, 3], hx.at[turn, 0]),
            (field.at[:, 0], hx.at[turn, 1]),
            (sy.at[turn, 0], hy.at[turn, 0]),
            (sy.at[turn, 1], hy.at[turn, 1]),
            (sz.at[turn, 0], hz.at[turn, 0]),
            (sz.at[turn, 1], hz.at[turn, 1]),
        )
        return [
            pltpu.make_async_remote_copy(
                src_ref=src,
                dst_ref=dst,
                send_sem=face_send.at[turn, n],
                recv_sem=face_recv.at[turn, n],
                device_id=faces[n],
                device_id_type=MESH,
            )
            for n, (src, dst) in enumerate(pairs)
        ]

    def halo_copies(turn, wide):
        rows = pl.ds(0, 6 if turn else 7)
        own = wide.at[pl.ds(BINS, BINS), rows]
        return [
            pltpu.make_async_remote_copy(
                src_ref=own,
                dst_ref=wide.at[pl.ds(start, BINS), rows],
                send_sem=halo_send.at[turn, n],
                recv_sem=halo_recv.at[turn, n],
                device_id=other,
                device_id_type=MESH,
            )
            for n, (start, other) in enumerate(((0, bin_right), (2 * BINS, bin_left)))
        ]

    def group_copy(turn, src, dst, other):
        return pltpu.make_async_remote_copy(
            src_ref=src,
            dst_ref=dst,
            send_sem=group_send.at[turn],
            recv_sem=group_recv.at[turn],
            device_id=other,
            device_id_type=MESH,
        )

    def group_start(turn, buffer, source):
        @pl.loop(1, group)
        def _(k):
            other = lax.rem(me + k, group)
            group_copy(turn, source(other), buffer.at[me], in_group(other)).start()

    def group_all(turn, buffer):
        most = buffer.at[pl.ds(0, group - 1)]
        return group_copy(turn, most, most, in_group(lax.rem(me + 1, group)))

    def gathered(buffer):
        out = []
        for t in range(tiles):
            total = buffer[t * per_tile]
            for s in range(t * per_tile + 1, min(group, (t + 1) * per_tile)):
                total = total + buffer[s]
            out.append(total)
        return jnp.concatenate(out, axis=1) if tiles > 1 else out[0]

    loads[2].wait()
    pack_y(0, fluid)
    pack_z(0, fluid)
    fluid_parts[...] = stacked(fluid[...].reshape(96, 128))

    for copy in loads[3:]:
        copy.wait()
    for c in range(3):
        wide1[BINS : 2 * BINS, c, :] = pos[c]
        wide1[BINS : 2 * BINS, 3 + c, :] = vel[c]
    count_rows = jnp.zeros((16, 128), i32)
    for b in range(BINS):
        count_rows = jnp.where(row16 == b, counts[b], count_rows)
    occupied = jnp.where(lane16 < count_rows, 1.0, 0.0).astype(f32)
    wide1[BINS : 2 * BINS, 6, :] = wts[...] * occupied
    wide1[BINS : 2 * BINS, 7, :] = occupied

    pl.semaphore_wait(barrier, group - 1 + 4)

    halo1 = halo_copies(0, wide1)
    for copy in halo1:
        copy.start()
    group_start(0, req, lambda other: req.at[me])
    faces0 = face_copies(0, fluid)
    for copy in faces0:
        copy.start()

    def prepare(wide, slot, scale, own):
        tile = wide[slot]
        carried = wide1[slot, 6:7, :] * scale
        v = jnp.where(row8 < 6, tile, jnp.where(row8 == 6, 1.0, 0.0)) * carried
        vh, vm, vl = parts(v)
        vals[slot] = jnp.concatenate([vh, vm, vl, jnp.zeros_like(vh)], axis=0).astype(bf16)
        y = jnp.where(row8 < 3, tile * ROOT_LOG2E, 0.0)
        norm = -0.5 * jnp.sum(y * y, axis=0, keepdims=True)
        h, m, l = parts(jnp.where(row8 == 3, norm, y))
        ones = jnp.where((row8 >= 4) & (row8 < 7), 1.0, h)
        aug[slot] = jnp.concatenate([ones, m, l, h, m, h], axis=0).astype(bf16)
        if own:
            high = jnp.where(row8 < 3, h, jnp.where(row8 == 3, 1.0, 0.0))
            low = jnp.where(row8 < 3, m, 0.0)
            lowest = jnp.where(row8 < 3, l, 0.0)
            norms = jnp.where(
                row8 == 4,
                h[3:4, :],
                jnp.where(row8 == 5, m[3:4, :], jnp.where(row8 == 6, l[3:4, :], high)),
            )
            own_aug[slot - BINS] = jnp.concatenate(
                [norms, high, high, low, low, lowest], axis=0
            ).astype(bf16)

    def prepare_own(wide):
        @pl.loop(BINS, 2 * BINS, unroll=8)
        def _(slot):
            prepare(wide, slot, 1.0, True)

    has_left = jnp.where(here > 0, 1.0, 0.0).astype(f32)
    has_right = jnp.where(here < devices - 1, 1.0, 0.0).astype(f32)

    def prepare_halo(wide, copies):
        for copy, first, scale in zip(copies, (0, 2 * BINS), (has_left, has_right)):
            copy.wait_recv()

            @pl.loop(first, first + BINS, unroll=8)
            def _(slot, scale=scale):
                prepare(wide, slot, scale, False)

    def near_of(b):
        slots = [b + BINS]
        for q in range(3):
            slots.append(jnp.where(lmask[q, b] != 0, b + BINS + loff[q, b], 3 * BINS))
        return slots

    def pair_kernel(b, slots, first):
        near = jnp.concatenate([aug[s] for s in slots], axis=1)
        exponent = lax.dot_general(
            near, own_aug[b], (((0,), (0,)), ((), ())), preferred_element_type=f32
        )
        pair = jnp.exp2(exponent)
        high = pair.astype(bf16)
        size = 128 * len(slots)
        pairs[b, first : first + size] = high
        pairs[b, 512 + first : 512 + first + size] = (pair - high.astype(f32)).astype(bf16)

    def contact_own():
        @pl.loop(0, BINS, unroll=16)
        def _(b):
            pair_kernel(b, [b + BINS], 0)

    def weigh(b):
        value = jnp.concatenate([vals[s] for s in near_of(b)], axis=1)
        total = jnp.dot(value, pairs[b, 0:512], preferred_element_type=f32)
        total = total + jnp.dot(value, pairs[b, 512:1024], preferred_element_type=f32)
        sums[b] = total[0:8] + total[8:16] + total[16:24]

    def contact():
        for b in range(BINS + 8):
            if b < BINS:
                pair_kernel(b, near_of(b)[1:], 128)
            if b >= 8:
                weigh(b - 8)

    def pushed_by(tile, total):
        net = tile * total[6:7, :] - total
        return STIFF * pltpu.roll(net, 3, 0) - DAMP * net

    def advanced(tile, force, seen):
        held = STEP * tile[7:8, :]
        new_v = tile + held * (force + (seen - tile))
        new_x = tile + held * pltpu.roll(new_v, 5, 0)
        return jnp.where(row8 < 3, new_x, jnp.where(row8 < 6, new_v, tile))

    aug[3 * BINS] = jnp.zeros((48, 128), bf16)
    vals[3 * BINS] = jnp.zeros((32, 128), bf16)
    prepare_own(wide1)
    contact_own()

    group_all(0, req).wait_recv()
    asked_all = gathered(req)
    wide_lanes = 128 * tiles
    cell = asked_all[1:2, :]
    lane_hot[...] = jnp.where(
        iota((128, wide_lanes), 0) == (cell & 127), 1.0, 0.0
    ).astype(bf16)
    row_hot[...] = jnp.where(
        (iota((32, wide_lanes), 0) == (cell >> 7)) & (asked_all[0:1, :] == me), 1.0, 0.0
    ).astype(f32)
    at_lane = jnp.dot(
        fluid_parts[...], lane_hot[...], preferred_element_type=f32
    )
    at_lane = at_lane[0:96] + at_lane[96:192] + at_lane[192:288]
    reply = jnp.zeros((8, wide_lanes), f32)
    wide_row = iota((8, wide_lanes), 0)
    for c in range(3):
        picked = jnp.sum(at_lane[32 * c : 32 * c + 32] * row_hot[...], axis=0, keepdims=True)
        reply = jnp.where(wide_row == 3 + c, picked, reply)
    for t in range(tiles):
        answer[t] = reply[:, 128 * t : 128 * t + 128]
    ans[me] = answer[lax.div(me, per_tile)]
    group_start(1, ans, lambda other: answer.at[lax.div(other, per_tile)])

    in_x = [jnp.where(g, 1.0, 0.0).astype(f32) for g in (gx > 0, gx < ngx - 1)]
    in_y = [jnp.where(g, 1.0, 0.0).astype(f32) for g in (gy > 0, gy < ngy - 1)]
    in_z = [jnp.where(g, 1.0, 0.0).astype(f32) for g in (gz > 0, gz < ngz - 1)]

    def laplace_inside(field, c, x):
        tile = field[c, x]
        total = -6.0 * tile
        if x > 0:
            total = total + field[c, x - 1]
        if x < 3:
            total = total + field[c, x + 1]
        total = total + jnp.where(row8 == 0, 0.0, pltpu.roll(tile, 1, 0))
        total = total + jnp.where(row8 == 7, 0.0, pltpu.roll(tile, 7, 0))
        total = total + jnp.where(lane8 == 0, 0.0, pltpu.roll(tile, 1, 1))
        return total + jnp.where(lane8 == 127, 0.0, pltpu.roll(tile, 127, 1))

    def laplace_edges(turn, c, x):
        k = c * 4 + x
        y0, y7 = hy[turn, 0, k : k + 1, :] * in_y[0], hy[turn, 1, k : k + 1, :] * in_y[1]
        z0, z127 = hz[turn, 0] * in_z[0], hz[turn, 1] * in_z[1]
        total = jnp.where(row8 == 0, y0, jnp.where(row8 == 7, y7, 0.0))
        total = total + jnp.where(
            lane8 == 0, z0[:, k : k + 1], jnp.where(lane8 == 127, z127[:, k : k + 1], 0.0)
        )
        if x == 0:
            total = total + hx[turn, 0, c] * in_x[0]
        if x == 3:
            total = total + hx[turn, 1, c] * in_x[1]
        return total

    prepare_halo(wide1, halo1)

    contact()

    drawn = jnp.zeros((8, 128), f32)
    for b in range(BINS):
        tile = wide1[BINS + b]
        force = pushed_by(tile, sums[b])
        held = STEP * tile[7:8, :]
        term = jnp.where(row8 == 6, 2.0 - held, held * (tile - force) - 2.0 * tile)
        drawn = jnp.where(
            lane8 == b, jnp.sum(tile[6:7, :] * term, axis=1, keepdims=True), drawn
        )
        sums[b] = force
    dep[me] = pltpu.roll(drawn, first_lane, 1)
    group_start(2, dep, lambda other: dep.at[me])

    for copy in faces0:
        copy.wait_recv()
    for c in range(3):
        for x in range(4):
            rate_buf[c, x] = VISC * (laplace_inside(fluid, c, x) + laplace_edges(0, c, x))

    group_all(1, ans).wait_recv()
    seen = ans[0]
    for s in range(1, group):
        seen = seen + ans[s]
    seen = pltpu.roll(seen, lax.rem(128 - first_lane, 128), 1)
    for b in range(BINS):
        seen_b = jnp.broadcast_to(seen[:, b : b + 1], (8, 128))
        wide2[BINS + b] = advanced(wide1[BINS + b], sums[b], seen_b)
    halo2 = halo_copies(1, wide2)
    for copy in halo2:
        copy.start()
    prepare_own(wide2)
    contact_own()

    group_all(2, dep).wait_recv()
    drawn_all = gathered(dep)
    there = [answer[t] for t in range(tiles)]
    there = jnp.concatenate(there, axis=1) if tiles > 1 else there[0]
    pushed = -COUPLING * (drawn_all[6:7, :] * there + drawn_all)
    spread = jnp.concatenate(
        [pushed[3 + c : 4 + c, :] * row_hot[...] for c in range(3)], axis=0
    )
    source = lax.dot_general(
        stacked(spread), lane_hot[...], (((1,), (1,)), ((), ())), preferred_element_type=f32
    )
    source = source[0:96] + source[96:192] + source[192:288]
    first_buf[...] = rate_buf[...] + source.reshape(3, 4, 8, 128)
    faces1 = face_copies(1, first_buf)
    pack_z(1, first_buf)
    for copy in (*faces1[4:], *faces1[:2]):
        copy.start()
    pack_y(1, first_buf)
    for copy in faces1[2:4]:
        copy.start()
    for c in range(3):
        for x in range(4):
            rate_buf[c, x] = (
                fluid[c, x] + first_buf[c, x] + (0.5 * VISC) * laplace_inside(first_buf, c, x)
            )

    prepare_halo(wide2, halo2)

    contact()

    for b in range(BINS):
        tile, seen_b = wide2[BINS + b], jnp.broadcast_to(seen[:, b : b + 1], (8, 128))
        sums[b] = advanced(tile, pushed_by(tile, sums[b]), seen_b)
    for c in range(3):
        pos_out[c] = sums[:, c, :]
        vel_out[c] = sums[:, 3 + c, :]

    for copy in faces1:
        copy.wait_recv()
    for c in range(3):
        for x in range(4):
            fluid_out[c, x] = rate_buf[c, x] + (0.5 * VISC) * laplace_edges(1, c, x)

    for copy in (*halo1, *faces0, *halo2, *faces1):
        copy.wait_send()
    for turn, buffer in enumerate((req, ans, dep)):
        group_all(turn, buffer).wait_send()


def write_out(*refs):
    sems = refs[-1]
    copies = [pltpu.make_async_copy(refs[n], refs[3 + n], sems.at[n]) for n in range(3)]
    for copy in copies:
        copy.start()
    for copy in copies:
        copy.wait()


def local(sizes, pos, vel, wts, counts, loff, lmask, bbox, bcell, fluid):
    group = sizes[0] * sizes[1]
    tiles = -(-group * BINS // 128)
    vmem, anywhere = pl.BlockSpec(memory_space=pltpu.VMEM), pl.BlockSpec(memory_space=pltpu.HBM)
    dma = pltpu.SemaphoreType.DMA
    args = (pos, vel, wts, counts, loff.T, lmask.T, bbox.T, bcell, fluid)
    out_shape = (
        jax.ShapeDtypeStruct((3, BINS, 128), f32),
        jax.ShapeDtypeStruct((3, BINS, 128), f32),
        jax.ShapeDtypeStruct((3, 4, 8, 128), f32),
    )
    results = pl.pallas_call(
            functools.partial(kernel, sizes),
            out_shape=out_shape,
            in_specs=[anywhere] * 9,
            out_specs=(vmem,) * 3,
            scratch_shapes=[
                pltpu.VMEM((3, BINS, 128), f32),
                pltpu.VMEM((3, BINS, 128), f32),
                pltpu.VMEM((BINS, 128), f32),
                pltpu.SMEM((BINS,), i32),
                pltpu.SMEM((3, BINS), i32),
                pltpu.SMEM((3, BINS), i32),
                pltpu.SMEM((1, BINS), i32),
                pltpu.SMEM((BINS,), i32),
                pltpu.VMEM((3, 4, 8, 128), f32),
                pltpu.VMEM((3 * BINS, 8, 128), f32),
                pltpu.VMEM((3 * BINS, 8, 128), f32),
                pltpu.VMEM((BINS, 48, 128), bf16),
                pltpu.VMEM((3 * BINS + 1, 48, 128), bf16),
                pltpu.VMEM((3 * BINS + 1, 32, 128), bf16),
                pltpu.VMEM((BINS, 8, 128), f32),
                pltpu.VMEM((BINS, 1024, 128), bf16),
                pltpu.VMEM((group, 8, 128), i32),
                pltpu.VMEM((tiles, 8, 128), f32),
                pltpu.VMEM((group, 8, 128), f32),
                pltpu.VMEM((group, 8, 128), f32),
                pltpu.VMEM((128, 128 * tiles), bf16),
                pltpu.VMEM((32, 128 * tiles), f32),
                pltpu.VMEM((288, 128), bf16),
                pltpu.VMEM((3, 4, 8, 128), f32),
                pltpu.VMEM((3, 4, 8, 128), f32),
                pltpu.VMEM((2, 2, 3, 8, 128), f32),
                pltpu.VMEM((2, 2, 16, 128), f32),
                pltpu.VMEM((2, 2, 8, 128), f32),
                pltpu.VMEM((2, 2, 16, 128), f32),
                pltpu.VMEM((2, 2, 8, 128), f32),
                dma((9,)),
                dma((2, 2)),
                dma((2, 2)),
                dma((3,)),
                dma((3,)),
                dma((2, 6)),
                dma((2, 6)),
            ],
            compiler_params=pltpu.CompilerParams(
                collective_id=0, has_side_effects=True, vmem_limit_bytes=16 * 2**20
            ),
            name="bed_step",
        )(*(pltpu.with_memory_space_constraint(x, pltpu.HBM) for x in args))
    return tuple(pl.pallas_call(
        write_out,
        out_shape=out_shape,
        in_specs=[vmem] * 3,
        out_specs=(anywhere,) * 3,
        scratch_shapes=[dma((3,))],
        compiler_params=pltpu.CompilerParams(vmem_limit_bytes=4 * 2**20),
        name="out_write",
    )(*results))


def solution(mesh):
    sizes = tuple(mesh.shape[a] for a in ("gx", "gy", "gz"))
    bins = ("gx", "gy", "gz")
    in_specs = (
        P(None, bins, None),
        P(None, bins, None),
        P(bins, None),
        P(bins),
        P(bins, None),
        P(bins, None),
        P(bins, None),
        P(bins),
        P(None, "gx", "gy", "gz"),
    )
    out_specs = (P(None, bins, None), P(None, bins, None), P(None, "gx", "gy", "gz"))
    return jax.shard_map(
        functools.partial(local, sizes),
        mesh=mesh,
        in_specs=in_specs,
        out_specs=out_specs,
        check_vma=False,
    )
```

```python
import functools

import jax
import jax.numpy as jnp
from jax import lax
from jax.experimental import pallas as pl
from jax.experimental.pallas import tpu as pltpu
from jax.sharding import PartitionSpec as P

f32, bf16, i32 = jnp.float32, jnp.bfloat16, jnp.int32
MESH = pl.DeviceIdType.MESH
BINS = 16
STEP, STIFF, DAMP, COUPLING, VISC = 0.1, 0.05, 0.05, 0.004, 0.12
ROOT_LOG2E = 1.4426950408889634**0.5


def iota(shape, dim):
    return lax.broadcasted_iota(i32, shape, dim)


def parts(x):
    high = x.astype(bf16).astype(f32)
    rest = x - high
    middle = rest.astype(bf16).astype(f32)
    return high, middle, rest - middle


def stacked(x):
    return jnp.concatenate([p.astype(bf16) for p in parts(x)], axis=0)


def kernel(
    sizes,
    pos_in,
    vel_in,
    wts_in,
    counts_in,
    loff_in,
    lmask_in,
    bbox_in,
    bcell_in,
    fluid_in,
    pos_out,
    vel_out,
    fluid_out,
    pos,
    vel,
    wts,
    counts,
    loff,
    lmask,
    bbox,
    bcell,
    fluid,
    wide1,
    wide2,
    own_aug,
    aug,
    vals,
    sums,
    pairs,
    req,
    answer,
    ans,
    dep,
    lane_hot,
    row_hot,
    fluid_parts,
    rate_buf,
    first_buf,
    hx,
    hy,
    hz,
    sy,
    sz,
    load_sem,
    halo_send,
    halo_recv,
    group_send,
    group_recv,
    face_send,
    face_recv,
):
    ngx, ngy, ngz = sizes
    group, devices = ngx * ngy, ngx * ngy * ngz
    tiles = -(-group * BINS // 128)
    per_tile = 128 // BINS
    gx, gy, gz = (lax.axis_index(a) for a in ("gx", "gy", "gz"))
    me = gx * ngy + gy
    here = me * ngz + gz

    def in_group(g):
        return (lax.div(g, ngy), lax.rem(g, ngy), gz)

    def at(n):
        g = lax.div(n, ngz)
        return (lax.div(g, ngy), lax.rem(g, ngy), lax.rem(n, ngz))

    bin_right, bin_left = at(lax.rem(here + 1, devices)), at(lax.rem(here + devices - 1, devices))
    faces = (
        (lax.rem(gx + 1, ngx), gy, gz),
        (lax.rem(gx + ngx - 1, ngx), gy, gz),
        (gx, lax.rem(gy + 1, ngy), gz),
        (gx, lax.rem(gy + ngy - 1, ngy), gz),
        (gx, gy, lax.rem(gz + 1, ngz)),
        (gx, gy, lax.rem(gz + ngz - 1, ngz)),
    )

    barrier = pltpu.get_barrier_semaphore()

    for other in (bin_right, bin_left, faces[4], faces[5]):
        pl.semaphore_signal(barrier, inc=1, device_id=other, device_id_type=MESH)

    @pl.loop(1, group)
    def _(k):
        pl.semaphore_signal(
            barrier, inc=1, device_id=in_group(lax.rem(me + k, group)), device_id_type=MESH
        )

    loads = [
        pltpu.make_async_copy(src, dst, load_sem.at[n])
        for n, (src, dst) in enumerate(
            (
                (bbox_in, bbox),
                (bcell_in, bcell),
                (fluid_in, fluid),
                (pos_in, pos),
                (vel_in, vel),
                (counts_in, counts),
                (wts_in, wts),
                (loff_in, loff),
                (lmask_in, lmask),
            )
        )
    ]
    for copy in loads:
        copy.start()

    row8, lane8 = iota((8, 128), 0), iota((8, 128), 1)
    row16, lane16 = iota((16, 128), 0), iota((16, 128), 1)

    loads[0].wait()
    loads[1].wait()
    asked = jnp.zeros((8, 128), i32)
    first_lane = lax.rem(me, per_tile) * BINS
    for b in range(BINS):
        asked = jnp.where(
            lane8 == first_lane + b,
            jnp.where(row8 == 0, bbox[0, b], jnp.where(row8 == 1, bcell[b], 0)),
            asked,
        )
    req[me] = asked

    def pack_y(turn, field):
        for side, edge in enumerate((7, 0)):
            rows = jnp.zeros((16, 128), f32)
            for k in range(12):
                rows = jnp.where(row16 == k, field[k // 4, k % 4, edge : edge + 1, :], rows)
            sy[turn, side] = rows

    def pack_z(turn, field):
        for side, edge in enumerate((127, 0)):
            lanes = jnp.zeros((8, 128), f32)
            for k in range(12):
                tile = field[k // 4, k % 4]
                lanes = jnp.where(lane8 == k, tile[:, edge : edge + 1], lanes)
            sz[turn, side] = lanes

    def face_copies(turn, field):
        pairs = (
            (field.at[:, 3], hx.at[turn, 0]),
            (field.at[:, 0], hx.at[turn, 1]),
            (sy.at[turn, 0], hy.at[turn, 0]),
            (sy.at[turn, 1], hy.at[turn, 1]),
            (sz.at[turn, 0], hz.at[turn, 0]),
            (sz.at[turn, 1], hz.at[turn, 1]),
        )
        return [
            pltpu.make_async_remote_copy(
                src_ref=src,
                dst_ref=dst,
                send_sem=face_send.at[turn, n],
                recv_sem=face_recv.at[turn, n],
                device_id=faces[n],
                device_id_type=MESH,
            )
            for n, (src, dst) in enumerate(pairs)
        ]

    half = BINS // 2

    def halo_copies(turn, wide):
        rows = pl.ds(0, 6 if turn else 7)
        return [
            pltpu.make_async_remote_copy(
                src_ref=wide.at[pl.ds(BINS + part * half, half), rows],
                dst_ref=wide.at[pl.ds(start + part * half, half), rows],
                send_sem=halo_send.at[turn, 2 * part + n],
                recv_sem=halo_recv.at[turn, 2 * part + n],
                device_id=other,
                device_id_type=MESH,
            )
            for part in range(2)
            for n, (start, other) in enumerate(((0, bin_right), (2 * BINS, bin_left)))
        ]

    def group_copy(turn, src, dst, other):
        return pltpu.make_async_remote_copy(
            src_ref=src,
            dst_ref=dst,
            send_sem=group_send.at[turn],
            recv_sem=group_recv.at[turn],
            device_id=other,
            device_id_type=MESH,
        )

    group_rows = (pl.ds(0, 2), pl.ds(3, 3), pl.ds(3, 4))

    def group_start(turn, buffer, source):
        rows = group_rows[turn]

        @pl.loop(1, group)
        def _(k):
            other = lax.rem(me + k, group)
            group_copy(
                turn, source(other).at[rows], buffer.at[me, rows], in_group(other)
            ).start()

    def group_all(turn, buffer):
        most = buffer.at[pl.ds(0, group - 1), group_rows[turn]]
        return group_copy(turn, most, most, in_group(lax.rem(me + 1, group)))

    def gathered(buffer):
        out = []
        for t in range(tiles):
            total = buffer[t * per_tile]
            for s in range(t * per_tile + 1, min(group, (t + 1) * per_tile)):
                total = total + buffer[s]
            out.append(total)
        return jnp.concatenate(out, axis=1) if tiles > 1 else out[0]

    loads[2].wait()
    pack_y(0, fluid)
    pack_z(0, fluid)
    fluid_parts[...] = stacked(fluid[...].reshape(96, 128))

    for copy in loads[3:]:
        copy.wait()
    for c in range(3):
        wide1[BINS : 2 * BINS, c, :] = pos[c]
        wide1[BINS : 2 * BINS, 3 + c, :] = vel[c]
    count_rows = jnp.zeros((16, 128), i32)
    for b in range(BINS):
        count_rows = jnp.where(row16 == b, counts[b], count_rows)
    occupied = jnp.where(lane16 < count_rows, 1.0, 0.0).astype(f32)
    wide1[BINS : 2 * BINS, 6, :] = wts[...] * occupied
    wide1[BINS : 2 * BINS, 7, :] = occupied

    pl.semaphore_wait(barrier, group - 1 + 4)

    halo1 = halo_copies(0, wide1)
    for copy in halo1:
        copy.start()
    group_start(0, req, lambda other: req.at[me])
    faces0 = face_copies(0, fluid)
    for copy in faces0:
        copy.start()

    def prepare(wide, slot, scale, own):
        tile = wide[slot]
        carried = wide1[slot, 6:7, :] * scale
        v = jnp.where(row8 < 6, tile, jnp.where(row8 == 6, 1.0, 0.0)) * carried
        vh, vm, vl = parts(v)
        vals[slot] = jnp.concatenate([vh, vm, vl, jnp.zeros_like(vh)], axis=0).astype(bf16)
        y = jnp.where(row8 < 3, tile * ROOT_LOG2E, 0.0)
        norm = -0.5 * jnp.sum(y * y, axis=0, keepdims=True)
        h, m, l = parts(jnp.where(row8 == 3, norm, y))
        ones = jnp.where((row8 >= 4) & (row8 < 7), 1.0, h)
        aug[slot] = jnp.concatenate([ones, m, l, h, m, h], axis=0).astype(bf16)
        if own:
            high = jnp.where(row8 < 3, h, jnp.where(row8 == 3, 1.0, 0.0))
            low = jnp.where(row8 < 3, m, 0.0)
            lowest = jnp.where(row8 < 3, l, 0.0)
            norms = jnp.where(
                row8 == 4,
                h[3:4, :],
                jnp.where(row8 == 5, m[3:4, :], jnp.where(row8 == 6, l[3:4, :], high)),
            )
            own_aug[slot - BINS] = jnp.concatenate(
                [norms, high, high, low, low, lowest], axis=0
            ).astype(bf16)

    def prepare_own(wide):
        @pl.loop(BINS, 2 * BINS, unroll=8)
        def _(slot):
            prepare(wide, slot, 1.0, True)

    has_left = jnp.where(here > 0, 1.0, 0.0).astype(f32)
    has_right = jnp.where(here < devices - 1, 1.0, 0.0).astype(f32)

    def prepare_halo(wide, copies):
        for n, copy in enumerate(copies):
            first, scale = ((0, has_left), (2 * BINS, has_right))[n % 2]
            copy.wait_recv()

            @pl.loop(0, half, unroll=half)
            def _(b, first=first + (n // 2) * half, scale=scale):
                prepare(wide, first + b, scale, False)

    def near_of(b):
        slots = [b + BINS]
        for q in range(3):
            slots.append(jnp.where(lmask[q, b] != 0, b + BINS + loff[q, b], 3 * BINS))
        return slots

    def pair_kernel(b, slots, first):
        near = jnp.concatenate([aug[s] for s in slots], axis=1)
        exponent = lax.dot_general(
            near, own_aug[b], (((0,), (0,)), ((), ())), preferred_element_type=f32
        )
        pair = jnp.exp2(exponent)
        high = pair.astype(bf16)
        size = 128 * len(slots)
        pairs[b, first : first + size] = high
        pairs[b, 512 + first : 512 + first + size] = (pair - high.astype(f32)).astype(bf16)

    def contact_own():
        @pl.loop(0, BINS, unroll=16)
        def _(b):
            pair_kernel(b, [b + BINS], 0)

    def weigh(b):
        value = jnp.concatenate([vals[s] for s in near_of(b)], axis=1)
        total = jnp.dot(value, pairs[b, 0:512], preferred_element_type=f32)
        total = total + jnp.dot(value, pairs[b, 512:1024], preferred_element_type=f32)
        sums[b] = total[0:8] + total[8:16] + total[16:24]

    def contact():
        for b in range(BINS + 8):
            if b < BINS:
                pair_kernel(b, near_of(b)[1:], 128)
            if b >= 8:
                weigh(b - 8)

    def pushed_by(tile, total):
        net = tile * total[6:7, :] - total
        return STIFF * pltpu.roll(net, 3, 0) - DAMP * net

    def advanced(tile, force, seen):
        held = STEP * tile[7:8, :]
        new_v = tile + held * (force + (seen - tile))
        new_x = tile + held * pltpu.roll(new_v, 5, 0)
        return jnp.where(row8 < 3, new_x, jnp.where(row8 < 6, new_v, tile))

    aug[3 * BINS] = jnp.zeros((48, 128), bf16)
    vals[3 * BINS] = jnp.zeros((32, 128), bf16)
    prepare_own(wide1)
    contact_own()

    group_all(0, req).wait_recv()
    asked_all = gathered(req)
    wide_lanes = 128 * tiles
    cell = asked_all[1:2, :]
    lane_hot[...] = jnp.where(
        iota((128, wide_lanes), 0) == (cell & 127), 1.0, 0.0
    ).astype(bf16)
    row_hot[...] = jnp.where(
        (iota((32, wide_lanes), 0) == (cell >> 7)) & (asked_all[0:1, :] == me), 1.0, 0.0
    ).astype(f32)
    at_lane = jnp.dot(
        fluid_parts[...], lane_hot[...], preferred_element_type=f32
    )
    at_lane = at_lane[0:96] + at_lane[96:192] + at_lane[192:288]
    reply = jnp.zeros((8, wide_lanes), f32)
    wide_row = iota((8, wide_lanes), 0)
    for c in range(3):
        picked = jnp.sum(at_lane[32 * c : 32 * c + 32] * row_hot[...], axis=0, keepdims=True)
        reply = jnp.where(wide_row == 3 + c, picked, reply)
    for t in range(tiles):
        answer[t] = reply[:, 128 * t : 128 * t + 128]
    ans[me] = answer[lax.div(me, per_tile)]
    group_start(1, ans, lambda other: answer.at[lax.div(other, per_tile)])

    in_x = [jnp.where(g, 1.0, 0.0).astype(f32) for g in (gx > 0, gx < ngx - 1)]
    in_y = [jnp.where(g, 1.0, 0.0).astype(f32) for g in (gy > 0, gy < ngy - 1)]
    in_z = [jnp.where(g, 1.0, 0.0).astype(f32) for g in (gz > 0, gz < ngz - 1)]

    def laplace_inside(field, c, x):
        tile = field[c, x]
        total = -6.0 * tile
        if x > 0:
            total = total + field[c, x - 1]
        if x < 3:
            total = total + field[c, x + 1]
        total = total + jnp.where(row8 == 0, 0.0, pltpu.roll(tile, 1, 0))
        total = total + jnp.where(row8 == 7, 0.0, pltpu.roll(tile, 7, 0))
        total = total + jnp.where(lane8 == 0, 0.0, pltpu.roll(tile, 1, 1))
        return total + jnp.where(lane8 == 127, 0.0, pltpu.roll(tile, 127, 1))

    def laplace_edges(turn, c, x):
        k = c * 4 + x
        y0, y7 = hy[turn, 0, k : k + 1, :] * in_y[0], hy[turn, 1, k : k + 1, :] * in_y[1]
        z0, z127 = hz[turn, 0] * in_z[0], hz[turn, 1] * in_z[1]
        total = jnp.where(row8 == 0, y0, jnp.where(row8 == 7, y7, 0.0))
        total = total + jnp.where(
            lane8 == 0, z0[:, k : k + 1], jnp.where(lane8 == 127, z127[:, k : k + 1], 0.0)
        )
        if x == 0:
            total = total + hx[turn, 0, c] * in_x[0]
        if x == 3:
            total = total + hx[turn, 1, c] * in_x[1]
        return total

    prepare_halo(wide1, halo1)

    contact()

    drawn = jnp.zeros((8, 128), f32)
    for b in range(BINS):
        tile = wide1[BINS + b]
        force = pushed_by(tile, sums[b])
        held = STEP * tile[7:8, :]
        term = jnp.where(row8 == 6, 2.0 - held, held * (tile - force) - 2.0 * tile)
        drawn = jnp.where(
            lane8 == b, jnp.sum(tile[6:7, :] * term, axis=1, keepdims=True), drawn
        )
        sums[b] = force
    dep[me] = pltpu.roll(drawn, first_lane, 1)
    group_start(2, dep, lambda other: dep.at[me])

    for copy in faces0:
        copy.wait_recv()
    for c in range(3):
        for x in range(4):
            rate_buf[c, x] = VISC * (laplace_inside(fluid, c, x) + laplace_edges(0, c, x))

    group_all(1, ans).wait_recv()
    seen = ans[0]
    for s in range(1, group):
        seen = seen + ans[s]
    seen = pltpu.roll(seen, lax.rem(128 - first_lane, 128), 1)
    for b in range(BINS):
        seen_b = jnp.broadcast_to(seen[:, b : b + 1], (8, 128))
        wide2[BINS + b] = advanced(wide1[BINS + b], sums[b], seen_b)
    halo2 = halo_copies(1, wide2)
    for copy in halo2:
        copy.start()
    prepare_own(wide2)
    contact_own()

    group_all(2, dep).wait_recv()
    drawn_all = gathered(dep)
    there = [answer[t] for t in range(tiles)]
    there = jnp.concatenate(there, axis=1) if tiles > 1 else there[0]
    pushed = -COUPLING * (drawn_all[6:7, :] * there + drawn_all)
    spread = jnp.concatenate(
        [pushed[3 + c : 4 + c, :] * row_hot[...] for c in range(3)], axis=0
    )
    source = lax.dot_general(
        stacked(spread), lane_hot[...], (((1,), (1,)), ((), ())), preferred_element_type=f32
    )
    source = source[0:96] + source[96:192] + source[192:288]
    first_buf[...] = rate_buf[...] + source.reshape(3, 4, 8, 128)
    faces1 = face_copies(1, first_buf)
    pack_z(1, first_buf)
    for copy in (*faces1[4:], *faces1[:2]):
        copy.start()
    pack_y(1, first_buf)
    for copy in faces1[2:4]:
        copy.start()
    for c in range(3):
        for x in range(4):
            rate_buf[c, x] = (
                fluid[c, x] + first_buf[c, x] + (0.5 * VISC) * laplace_inside(first_buf, c, x)
            )

    prepare_halo(wide2, halo2)

    contact()

    for b in range(BINS):
        tile, seen_b = wide2[BINS + b], jnp.broadcast_to(seen[:, b : b + 1], (8, 128))
        sums[b] = advanced(tile, pushed_by(tile, sums[b]), seen_b)
    for c in range(3):
        pos_out[c] = sums[:, c, :]
        vel_out[c] = sums[:, 3 + c, :]

    for copy in faces1:
        copy.wait_recv()
    for c in range(3):
        for x in range(4):
            fluid_out[c, x] = rate_buf[c, x] + (0.5 * VISC) * laplace_edges(1, c, x)

    for copy in (*halo1, *faces0, *halo2, *faces1):
        copy.wait_send()
    for turn, buffer in enumerate((req, ans, dep)):
        group_all(turn, buffer).wait_send()


def write_out(*refs):
    sems = refs[-1]
    copies = [pltpu.make_async_copy(refs[n], refs[3 + n], sems.at[n]) for n in range(3)]
    for copy in copies:
        copy.start()
    for copy in copies:
        copy.wait()


def local(sizes, pos, vel, wts, counts, loff, lmask, bbox, bcell, fluid):
    group = sizes[0] * sizes[1]
    tiles = -(-group * BINS // 128)
    vmem, anywhere = pl.BlockSpec(memory_space=pltpu.VMEM), pl.BlockSpec(memory_space=pltpu.HBM)
    dma = pltpu.SemaphoreType.DMA
    args = (pos, vel, wts, counts, loff.T, lmask.T, bbox.T, bcell, fluid)
    out_shape = (
        jax.ShapeDtypeStruct((3, BINS, 128), f32),
        jax.ShapeDtypeStruct((3, BINS, 128), f32),
        jax.ShapeDtypeStruct((3, 4, 8, 128), f32),
    )
    results = pl.pallas_call(
            functools.partial(kernel, sizes),
            out_shape=out_shape,
            in_specs=[anywhere] * 9,
            out_specs=(vmem,) * 3,
            scratch_shapes=[
                pltpu.VMEM((3, BINS, 128), f32),
                pltpu.VMEM((3, BINS, 128), f32),
                pltpu.VMEM((BINS, 128), f32),
                pltpu.SMEM((BINS,), i32),
                pltpu.SMEM((3, BINS), i32),
                pltpu.SMEM((3, BINS), i32),
                pltpu.SMEM((1, BINS), i32),
                pltpu.SMEM((BINS,), i32),
                pltpu.VMEM((3, 4, 8, 128), f32),
                pltpu.VMEM((3 * BINS, 8, 128), f32),
                pltpu.VMEM((3 * BINS, 8, 128), f32),
                pltpu.VMEM((BINS, 48, 128), bf16),
                pltpu.VMEM((3 * BINS + 1, 48, 128), bf16),
                pltpu.VMEM((3 * BINS + 1, 32, 128), bf16),
                pltpu.VMEM((BINS, 8, 128), f32),
                pltpu.VMEM((BINS, 1024, 128), bf16),
                pltpu.VMEM((group, 8, 128), i32),
                pltpu.VMEM((tiles, 8, 128), f32),
                pltpu.VMEM((group, 8, 128), f32),
                pltpu.VMEM((group, 8, 128), f32),
                pltpu.VMEM((128, 128 * tiles), bf16),
                pltpu.VMEM((32, 128 * tiles), f32),
                pltpu.VMEM((288, 128), bf16),
                pltpu.VMEM((3, 4, 8, 128), f32),
                pltpu.VMEM((3, 4, 8, 128), f32),
                pltpu.VMEM((2, 2, 3, 8, 128), f32),
                pltpu.VMEM((2, 2, 16, 128), f32),
                pltpu.VMEM((2, 2, 8, 128), f32),
                pltpu.VMEM((2, 2, 16, 128), f32),
                pltpu.VMEM((2, 2, 8, 128), f32),
                dma((9,)),
                dma((2, 4)),
                dma((2, 4)),
                dma((3,)),
                dma((3,)),
                dma((2, 6)),
                dma((2, 6)),
            ],
            compiler_params=pltpu.CompilerParams(
                collective_id=0, has_side_effects=True, vmem_limit_bytes=16 * 2**20
            ),
            name="bed_step",
        )(*(pltpu.with_memory_space_constraint(x, pltpu.HBM) for x in args))
    return tuple(pl.pallas_call(
        write_out,
        out_shape=out_shape,
        in_specs=[vmem] * 3,
        out_specs=(anywhere,) * 3,
        scratch_shapes=[dma((3,))],
        compiler_params=pltpu.CompilerParams(vmem_limit_bytes=4 * 2**20),
        name="out_write",
    )(*results))


def solution(mesh):
    sizes = tuple(mesh.shape[a] for a in ("gx", "gy", "gz"))
    bins = ("gx", "gy", "gz")
    in_specs = (
        P(None, bins, None),
        P(None, bins, None),
        P(bins, None),
        P(bins),
        P(bins, None),
        P(bins, None),
        P(bins, None),
        P(bins),
        P(None, "gx", "gy", "gz"),
    )
    out_specs = (P(None, bins, None), P(None, bins, None), P(None, "gx", "gy", "gz"))
    return jax.shard_map(
        functools.partial(local, sizes),
        mesh=mesh,
        in_specs=in_specs,
        out_specs=out_specs,
        check_vma=False,
    )
```

```python
import functools

import jax
import jax.numpy as jnp
from jax import lax
from jax.experimental import pallas as pl
from jax.experimental.pallas import tpu as pltpu
from jax.sharding import PartitionSpec as P

f32, bf16, i32 = jnp.float32, jnp.bfloat16, jnp.int32
MESH = pl.DeviceIdType.MESH
BINS = 16
STEP, STIFF, DAMP, COUPLING, VISC = 0.1, 0.05, 0.05, 0.004, 0.12
ROOT_LOG2E = 1.4426950408889634**0.5


def iota(shape, dim):
    return lax.broadcasted_iota(i32, shape, dim)


def parts(x):
    high = x.astype(bf16).astype(f32)
    rest = x - high
    middle = rest.astype(bf16).astype(f32)
    return high, middle, rest - middle


def stacked(x):
    return jnp.concatenate([p.astype(bf16) for p in parts(x)], axis=0)


def kernel(
    sizes,
    pos_in,
    vel_in,
    wts_in,
    counts_in,
    loff_in,
    lmask_in,
    bbox_in,
    bcell_in,
    fluid_in,
    pos_out,
    vel_out,
    fluid_out,
    pos,
    vel,
    wts,
    counts,
    loff,
    lmask,
    bbox,
    bcell,
    fluid,
    wide1,
    wide2,
    own_aug,
    aug,
    vals,
    sums,
    pairs,
    req,
    answer,
    ans,
    dep,
    lane_hot,
    row_hot,
    fluid_parts,
    rate_buf,
    first_buf,
    hx,
    hy,
    hz,
    sy,
    sz,
    load_sem,
    halo_send,
    halo_recv,
    group_send,
    group_recv,
    face_send,
    face_recv,
):
    ngx, ngy, ngz = sizes
    group, devices = ngx * ngy, ngx * ngy * ngz
    tiles = -(-group * BINS // 128)
    per_tile = 128 // BINS
    gx, gy, gz = (lax.axis_index(a) for a in ("gx", "gy", "gz"))
    me = gx * ngy + gy
    here = me * ngz + gz

    def in_group(g):
        return (lax.div(g, ngy), lax.rem(g, ngy), gz)

    def at(n):
        g = lax.div(n, ngz)
        return (lax.div(g, ngy), lax.rem(g, ngy), lax.rem(n, ngz))

    bin_right, bin_left = at(lax.rem(here + 1, devices)), at(lax.rem(here + devices - 1, devices))
    faces = (
        (lax.rem(gx + 1, ngx), gy, gz),
        (lax.rem(gx + ngx - 1, ngx), gy, gz),
        (gx, lax.rem(gy + 1, ngy), gz),
        (gx, lax.rem(gy + ngy - 1, ngy), gz),
        (gx, gy, lax.rem(gz + 1, ngz)),
        (gx, gy, lax.rem(gz + ngz - 1, ngz)),
    )

    barrier = pltpu.get_barrier_semaphore()

    for other in (bin_right, bin_left, faces[4], faces[5]):
        pl.semaphore_signal(barrier, inc=1, device_id=other, device_id_type=MESH)

    @pl.loop(1, group)
    def _(k):
        pl.semaphore_signal(
            barrier, inc=1, device_id=in_group(lax.rem(me + k, group)), device_id_type=MESH
        )

    loads = [
        pltpu.make_async_copy(src, dst, load_sem.at[n])
        for n, (src, dst) in enumerate(
            (
                (bbox_in, bbox),
                (bcell_in, bcell),
                (fluid_in, fluid),
                (pos_in, pos),
                (vel_in, vel),
                (counts_in, counts),
                (wts_in, wts),
                (loff_in, loff),
                (lmask_in, lmask),
            )
        )
    ]
    for copy in loads:
        copy.start()

    row8, lane8 = iota((8, 128), 0), iota((8, 128), 1)
    row16, lane16 = iota((16, 128), 0), iota((16, 128), 1)

    loads[0].wait()
    loads[1].wait()
    asked = jnp.zeros((8, 128), i32)
    first_lane = lax.rem(me, per_tile) * BINS
    for b in range(BINS):
        asked = jnp.where(
            lane8 == first_lane + b,
            jnp.where(row8 == 0, bbox[0, b], jnp.where(row8 == 1, bcell[b], 0)),
            asked,
        )
    req[me] = asked

    def pack_y(turn, field):
        for side, edge in enumerate((7, 0)):
            rows = jnp.zeros((16, 128), f32)
            for k in range(12):
                rows = jnp.where(row16 == k, field[k // 4, k % 4, edge : edge + 1, :], rows)
            sy[turn, side] = rows

    def pack_z(turn, field):
        for side, edge in enumerate((127, 0)):
            lanes = jnp.zeros((8, 128), f32)
            for k in range(12):
                tile = field[k // 4, k % 4]
                lanes = jnp.where(lane8 == k, tile[:, edge : edge + 1], lanes)
            sz[turn, side] = lanes

    def face_copies(turn, field):
        pairs = (
            (field.at[:, 3], hx.at[turn, 0]),
            (field.at[:, 0], hx.at[turn, 1]),
            (sy.at[turn, 0], hy.at[turn, 0]),
            (sy.at[turn, 1], hy.at[turn, 1]),
            (sz.at[turn, 0], hz.at[turn, 0]),
            (sz.at[turn, 1], hz.at[turn, 1]),
        )
        return [
            pltpu.make_async_remote_copy(
                src_ref=src,
                dst_ref=dst,
                send_sem=face_send.at[turn, n],
                recv_sem=face_recv.at[turn, n],
                device_id=faces[n],
                device_id_type=MESH,
            )
            for n, (src, dst) in enumerate(pairs)
        ]

    half = BINS // 2

    def halo_copies(turn, wide):
        rows = pl.ds(0, 6 if turn else 7)
        return [
            pltpu.make_async_remote_copy(
                src_ref=wide.at[pl.ds(BINS + part * half, half), rows],
                dst_ref=wide.at[pl.ds(start + part * half, half), rows],
                send_sem=halo_send.at[turn, 2 * part + n],
                recv_sem=halo_recv.at[turn, 2 * part + n],
                device_id=other,
                device_id_type=MESH,
            )
            for part in range(2)
            for n, (start, other) in enumerate(((0, bin_right), (2 * BINS, bin_left)))
        ]

    def group_copy(turn, src, dst, other):
        return pltpu.make_async_remote_copy(
            src_ref=src,
            dst_ref=dst,
            send_sem=group_send.at[turn],
            recv_sem=group_recv.at[turn],
            device_id=other,
            device_id_type=MESH,
        )

    group_rows = (pl.ds(0, 2), pl.ds(3, 3), pl.ds(3, 4))

    def group_start(turn, buffer, source):
        rows = group_rows[turn]

        for k in sorted(range(1, group), key=lambda k: -min(k % ngy, -k % ngy)):
            other = lax.rem(me + k, group)
            group_copy(
                turn, source(other).at[rows], buffer.at[me, rows], in_group(other)
            ).start()

    def group_all(turn, buffer):
        most = buffer.at[pl.ds(0, group - 1), group_rows[turn]]
        return group_copy(turn, most, most, in_group(lax.rem(me + 1, group)))

    def gathered(buffer):
        out = []
        for t in range(tiles):
            total = buffer[t * per_tile]
            for s in range(t * per_tile + 1, min(group, (t + 1) * per_tile)):
                total = total + buffer[s]
            out.append(total)
        return jnp.concatenate(out, axis=1) if tiles > 1 else out[0]

    loads[2].wait()
    pack_y(0, fluid)
    pack_z(0, fluid)
    fluid_parts[...] = stacked(fluid[...].reshape(96, 128))

    for copy in loads[3:]:
        copy.wait()
    for c in range(3):
        wide1[BINS : 2 * BINS, c, :] = pos[c]
        wide1[BINS : 2 * BINS, 3 + c, :] = vel[c]
    count_rows = jnp.zeros((16, 128), i32)
    for b in range(BINS):
        count_rows = jnp.where(row16 == b, counts[b], count_rows)
    occupied = jnp.where(lane16 < count_rows, 1.0, 0.0).astype(f32)
    wide1[BINS : 2 * BINS, 6, :] = wts[...] * occupied
    wide1[BINS : 2 * BINS, 7, :] = occupied

    pl.semaphore_wait(barrier, group - 1 + 4)

    halo1 = halo_copies(0, wide1)
    for copy in halo1:
        copy.start()
    group_start(0, req, lambda other: req.at[me])
    faces0 = face_copies(0, fluid)
    for copy in faces0:
        copy.start()

    def prepare(wide, slot, scale, own):
        tile = wide[slot]
        carried = wide1[slot, 6:7, :] * scale
        v = jnp.where(row8 < 6, tile, jnp.where(row8 == 6, 1.0, 0.0)) * carried
        vh, vm, vl = parts(v)
        vals[slot] = jnp.concatenate([vh, vm, vl, jnp.zeros_like(vh)], axis=0).astype(bf16)
        y = jnp.where(row8 < 3, tile * ROOT_LOG2E, 0.0)
        norm = -0.5 * jnp.sum(y * y, axis=0, keepdims=True)
        h, m, l = parts(jnp.where(row8 == 3, norm, y))
        ones = jnp.where((row8 >= 4) & (row8 < 7), 1.0, h)
        aug[slot] = jnp.concatenate([ones, m, l, h, m, h], axis=0).astype(bf16)
        if own:
            high = jnp.where(row8 < 3, h, jnp.where(row8 == 3, 1.0, 0.0))
            low = jnp.where(row8 < 3, m, 0.0)
            lowest = jnp.where(row8 < 3, l, 0.0)
            norms = jnp.where(
                row8 == 4,
                h[3:4, :],
                jnp.where(row8 == 5, m[3:4, :], jnp.where(row8 == 6, l[3:4, :], high)),
            )
            own_aug[slot - BINS] = jnp.concatenate(
                [norms, high, high, low, low, lowest], axis=0
            ).astype(bf16)

    def prepare_own(wide):
        @pl.loop(BINS, 2 * BINS, unroll=8)
        def _(slot):
            prepare(wide, slot, 1.0, True)

    has_left = jnp.where(here > 0, 1.0, 0.0).astype(f32)
    has_right = jnp.where(here < devices - 1, 1.0, 0.0).astype(f32)

    def prepare_halo(wide, copies):
        for n, copy in enumerate(copies):
            first, scale = ((0, has_left), (2 * BINS, has_right))[n % 2]
            copy.wait_recv()

            @pl.loop(0, half, unroll=half)
            def _(b, first=first + (n // 2) * half, scale=scale):
                prepare(wide, first + b, scale, False)

    def near_of(b):
        slots = [b + BINS]
        for q in range(3):
            slots.append(jnp.where(lmask[q, b] != 0, b + BINS + loff[q, b], 3 * BINS))
        return slots

    def pair_kernel(b, slots, first):
        near = jnp.concatenate([aug[s] for s in slots], axis=1)
        exponent = lax.dot_general(
            near, own_aug[b], (((0,), (0,)), ((), ())), preferred_element_type=f32
        )
        pair = jnp.exp2(exponent)
        high = pair.astype(bf16)
        size = 128 * len(slots)
        pairs[b, first : first + size] = high
        pairs[b, 512 + first : 512 + first + size] = (pair - high.astype(f32)).astype(bf16)

    def contact_own():
        @pl.loop(0, BINS, unroll=16)
        def _(b):
            pair_kernel(b, [b + BINS], 0)

    def weigh(b):
        value = jnp.concatenate([vals[s] for s in near_of(b)], axis=1)
        total = jnp.dot(value, pairs[b, 0:512], preferred_element_type=f32)
        total = total + jnp.dot(value, pairs[b, 512:1024], preferred_element_type=f32)
        sums[b] = total[0:8] + total[8:16] + total[16:24]

    def contact():
        for b in range(BINS + 8):
            if b < BINS:
                pair_kernel(b, near_of(b)[1:], 128)
            if b >= 8:
                weigh(b - 8)

    def pushed_by(tile, total):
        net = tile * total[6:7, :] - total
        return STIFF * pltpu.roll(net, 3, 0) - DAMP * net

    def advanced(tile, force, seen):
        held = STEP * tile[7:8, :]
        new_v = tile + held * (force + (seen - tile))
        new_x = tile + held * pltpu.roll(new_v, 5, 0)
        return jnp.where(row8 < 3, new_x, jnp.where(row8 < 6, new_v, tile))

    aug[3 * BINS] = jnp.zeros((48, 128), bf16)
    vals[3 * BINS] = jnp.zeros((32, 128), bf16)
    prepare_own(wide1)
    contact_own()

    group_all(0, req).wait_recv()
    asked_all = gathered(req)
    wide_lanes = 128 * tiles
    cell = asked_all[1:2, :]
    lane_hot[...] = jnp.where(
        iota((128, wide_lanes), 0) == (cell & 127), 1.0, 0.0
    ).astype(bf16)
    row_hot[...] = jnp.where(
        (iota((32, wide_lanes), 0) == (cell >> 7)) & (asked_all[0:1, :] == me), 1.0, 0.0
    ).astype(f32)
    at_lane = jnp.dot(
        fluid_parts[...], lane_hot[...], preferred_element_type=f32
    )
    at_lane = at_lane[0:96] + at_lane[96:192] + at_lane[192:288]
    reply = jnp.zeros((8, wide_lanes), f32)
    wide_row = iota((8, wide_lanes), 0)
    for c in range(3):
        picked = jnp.sum(at_lane[32 * c : 32 * c + 32] * row_hot[...], axis=0, keepdims=True)
        reply = jnp.where(wide_row == 3 + c, picked, reply)
    for t in range(tiles):
        answer[t] = reply[:, 128 * t : 128 * t + 128]
    ans[me] = answer[lax.div(me, per_tile)]
    group_start(1, ans, lambda other: answer.at[lax.div(other, per_tile)])

    in_x = [jnp.where(g, 1.0, 0.0).astype(f32) for g in (gx > 0, gx < ngx - 1)]
    in_y = [jnp.where(g, 1.0, 0.0).astype(f32) for g in (gy > 0, gy < ngy - 1)]
    in_z = [jnp.where(g, 1.0, 0.0).astype(f32) for g in (gz > 0, gz < ngz - 1)]

    def laplace_inside(field, c, x):
        tile = field[c, x]
        total = -6.0 * tile
        if x > 0:
            total = total + field[c, x - 1]
        if x < 3:
            total = total + field[c, x + 1]
        total = total + jnp.where(row8 == 0, 0.0, pltpu.roll(tile, 1, 0))
        total = total + jnp.where(row8 == 7, 0.0, pltpu.roll(tile, 7, 0))
        total = total + jnp.where(lane8 == 0, 0.0, pltpu.roll(tile, 1, 1))
        return total + jnp.where(lane8 == 127, 0.0, pltpu.roll(tile, 127, 1))

    def laplace_edges(turn, c, x):
        k = c * 4 + x
        y0, y7 = hy[turn, 0, k : k + 1, :] * in_y[0], hy[turn, 1, k : k + 1, :] * in_y[1]
        z0, z127 = hz[turn, 0] * in_z[0], hz[turn, 1] * in_z[1]
        total = jnp.where(row8 == 0, y0, jnp.where(row8 == 7, y7, 0.0))
        total = total + jnp.where(
            lane8 == 0, z0[:, k : k + 1], jnp.where(lane8 == 127, z127[:, k : k + 1], 0.0)
        )
        if x == 0:
            total = total + hx[turn, 0, c] * in_x[0]
        if x == 3:
            total = total + hx[turn, 1, c] * in_x[1]
        return total

    prepare_halo(wide1, halo1)

    contact()

    drawn = jnp.zeros((8, 128), f32)
    for b in range(BINS):
        tile = wide1[BINS + b]
        force = pushed_by(tile, sums[b])
        held = STEP * tile[7:8, :]
        term = jnp.where(row8 == 6, 2.0 - held, held * (tile - force) - 2.0 * tile)
        drawn = jnp.where(
            lane8 == b, jnp.sum(tile[6:7, :] * term, axis=1, keepdims=True), drawn
        )
        sums[b] = force
    dep[me] = pltpu.roll(drawn, first_lane, 1)
    group_start(2, dep, lambda other: dep.at[me])

    for copy in faces0:
        copy.wait_recv()
    for c in range(3):
        for x in range(4):
            rate_buf[c, x] = VISC * (laplace_inside(fluid, c, x) + laplace_edges(0, c, x))

    group_all(1, ans).wait_recv()
    seen = ans[0]
    for s in range(1, group):
        seen = seen + ans[s]
    seen = pltpu.roll(seen, lax.rem(128 - first_lane, 128), 1)
    for b in range(BINS):
        seen_b = jnp.broadcast_to(seen[:, b : b + 1], (8, 128))
        wide2[BINS + b] = advanced(wide1[BINS + b], sums[b], seen_b)
    halo2 = halo_copies(1, wide2)
    for copy in halo2:
        copy.start()
    prepare_own(wide2)
    contact_own()

    group_all(2, dep).wait_recv()
    drawn_all = gathered(dep)
    there = [answer[t] for t in range(tiles)]
    there = jnp.concatenate(there, axis=1) if tiles > 1 else there[0]
    pushed = -COUPLING * (drawn_all[6:7, :] * there + drawn_all)
    spread = jnp.concatenate(
        [pushed[3 + c : 4 + c, :] * row_hot[...] for c in range(3)], axis=0
    )
    source = lax.dot_general(
        stacked(spread), lane_hot[...], (((1,), (1,)), ((), ())), preferred_element_type=f32
    )
    source = source[0:96] + source[96:192] + source[192:288]
    first_buf[...] = rate_buf[...] + source.reshape(3, 4, 8, 128)
    faces1 = face_copies(1, first_buf)
    pack_z(1, first_buf)
    for copy in (*faces1[4:], *faces1[:2]):
        copy.start()
    pack_y(1, first_buf)
    for copy in faces1[2:4]:
        copy.start()
    for c in range(3):
        for x in range(4):
            rate_buf[c, x] = (
                fluid[c, x] + first_buf[c, x] + (0.5 * VISC) * laplace_inside(first_buf, c, x)
            )

    prepare_halo(wide2, halo2)

    contact()

    for b in range(BINS):
        tile, seen_b = wide2[BINS + b], jnp.broadcast_to(seen[:, b : b + 1], (8, 128))
        sums[b] = advanced(tile, pushed_by(tile, sums[b]), seen_b)
    for c in range(3):
        pos_out[c] = sums[:, c, :]
        vel_out[c] = sums[:, 3 + c, :]

    for copy in faces1:
        copy.wait_recv()
    for c in range(3):
        for x in range(4):
            fluid_out[c, x] = rate_buf[c, x] + (0.5 * VISC) * laplace_edges(1, c, x)

    for copy in (*halo1, *faces0, *halo2, *faces1):
        copy.wait_send()
    for turn, buffer in enumerate((req, ans, dep)):
        group_all(turn, buffer).wait_send()


def write_out(*refs):
    sems = refs[-1]
    copies = [pltpu.make_async_copy(refs[n], refs[3 + n], sems.at[n]) for n in range(3)]
    for copy in copies:
        copy.start()
    for copy in copies:
        copy.wait()


def local(sizes, pos, vel, wts, counts, loff, lmask, bbox, bcell, fluid):
    group = sizes[0] * sizes[1]
    tiles = -(-group * BINS // 128)
    vmem, anywhere = pl.BlockSpec(memory_space=pltpu.VMEM), pl.BlockSpec(memory_space=pltpu.HBM)
    dma = pltpu.SemaphoreType.DMA
    args = (pos, vel, wts, counts, loff.T, lmask.T, bbox.T, bcell, fluid)
    out_shape = (
        jax.ShapeDtypeStruct((3, BINS, 128), f32),
        jax.ShapeDtypeStruct((3, BINS, 128), f32),
        jax.ShapeDtypeStruct((3, 4, 8, 128), f32),
    )
    results = pl.pallas_call(
            functools.partial(kernel, sizes),
            out_shape=out_shape,
            in_specs=[anywhere] * 9,
            out_specs=(vmem,) * 3,
            scratch_shapes=[
                pltpu.VMEM((3, BINS, 128), f32),
                pltpu.VMEM((3, BINS, 128), f32),
                pltpu.VMEM((BINS, 128), f32),
                pltpu.SMEM((BINS,), i32),
                pltpu.SMEM((3, BINS), i32),
                pltpu.SMEM((3, BINS), i32),
                pltpu.SMEM((1, BINS), i32),
                pltpu.SMEM((BINS,), i32),
                pltpu.VMEM((3, 4, 8, 128), f32),
                pltpu.VMEM((3 * BINS, 8, 128), f32),
                pltpu.VMEM((3 * BINS, 8, 128), f32),
                pltpu.VMEM((BINS, 48, 128), bf16),
                pltpu.VMEM((3 * BINS + 1, 48, 128), bf16),
                pltpu.VMEM((3 * BINS + 1, 32, 128), bf16),
                pltpu.VMEM((BINS, 8, 128), f32),
                pltpu.VMEM((BINS, 1024, 128), bf16),
                pltpu.VMEM((group, 8, 128), i32),
                pltpu.VMEM((tiles, 8, 128), f32),
                pltpu.VMEM((group, 8, 128), f32),
                pltpu.VMEM((group, 8, 128), f32),
                pltpu.VMEM((128, 128 * tiles), bf16),
                pltpu.VMEM((32, 128 * tiles), f32),
                pltpu.VMEM((288, 128), bf16),
                pltpu.VMEM((3, 4, 8, 128), f32),
                pltpu.VMEM((3, 4, 8, 128), f32),
                pltpu.VMEM((2, 2, 3, 8, 128), f32),
                pltpu.VMEM((2, 2, 16, 128), f32),
                pltpu.VMEM((2, 2, 8, 128), f32),
                pltpu.VMEM((2, 2, 16, 128), f32),
                pltpu.VMEM((2, 2, 8, 128), f32),
                dma((9,)),
                dma((2, 4)),
                dma((2, 4)),
                dma((3,)),
                dma((3,)),
                dma((2, 6)),
                dma((2, 6)),
            ],
            compiler_params=pltpu.CompilerParams(
                collective_id=0, has_side_effects=True, vmem_limit_bytes=16 * 2**20
            ),
            name="bed_step",
        )(*(pltpu.with_memory_space_constraint(x, pltpu.HBM) for x in args))
    return tuple(pl.pallas_call(
        write_out,
        out_shape=out_shape,
        in_specs=[vmem] * 3,
        out_specs=(anywhere,) * 3,
        scratch_shapes=[dma((3,))],
        compiler_params=pltpu.CompilerParams(vmem_limit_bytes=4 * 2**20),
        name="out_write",
    )(*results))


def solution(mesh):
    sizes = tuple(mesh.shape[a] for a in ("gx", "gy", "gz"))
    bins = ("gx", "gy", "gz")
    in_specs = (
        P(None, bins, None),
        P(None, bins, None),
        P(bins, None),
        P(bins),
        P(bins, None),
        P(bins, None),
        P(bins, None),
        P(bins),
        P(None, "gx", "gy", "gz"),
    )
    out_specs = (P(None, bins, None), P(None, bins, None), P(None, "gx", "gy", "gz"))
    return jax.shard_map(
        functools.partial(local, sizes),
        mesh=mesh,
        in_specs=in_specs,
        out_specs=out_specs,
        check_vma=False,
    )
```
